32 devices in a mesh: labels: 8 (over z, y), heads: 4 (over x, core).
Axes of the slice: x: 2, y: 2, z: 4, core: 2. Of those that a mesh axis runs over, the one named last changes fastest.
Arguments:
- hidden_in: bfloat16 [4096, 768], P('labels', 'heads'), may hold values from -6 to 6
- w_up: bfloat16 [768, 3072], P(None, 'heads'), may hold values from -0.21875 to 0.21875
- w_down: bfloat16 [3072, 768], P('heads'), may hold values from -0.109375 to 0.109375
- norm_gain: float32 [768], replicated, may hold values from 0.25 to 1.75
- title_length: int32 [256], P('labels'), may hold values from 1 to 16
- label_leaf: int32 [256], P('labels'), may hold values from 0 to 63, as said below
- leaf_parent: int32 [64], P('labels'), may hold values from 0 to 15
Outputs:
- label_embed: bfloat16 [256, 768], P('labels')
- leaf_centers: float32 [64, 768], P('labels', 'heads')
- parent_sums: float32 [16, 768], P('labels', 'heads')
The draws below stay inside these ranges and needn't reach their ends.
Inputs may be any that keep to these rules, and one draw needn't show every extreme that they name: `label_leaf`: leaf l belongs to owner l // 8. The 32 labels of one device (an aligned block of 32 labels) name leaves of any one owner at most 8 times; in every draw one owner is named exactly 8 times by every device.
All inputs are finite; a program needn't handle non-finite values.
Results may differ from the reference program's by a relative error of at most 0.009.
Values may be sent and summed in bfloat16 or wider, within the bound.
No kernel may reach another device: no remote copies, remote signals or barrier semaphores. Data moves between devices by JAX's collectives and lax.ppermute only.
A program may use at most 64 MiB of HBM per device.

```python
import math
import jax
import jax.numpy as jnp
from jax import lax

D = 768
FF = 3072
SEQ = 16
LAB_DEV = 32
LEAF_DEV = 8
LABELS = 256
LEAVES = 64
PARENTS = 16
CAP = 8
N_HEADS = 4


def draw_label_leaf(key, part):
    owner_total = LABELS // LAB_DEV
    hot_owner = jax.random.randint(jax.random.fold_in(key, 7), (), 0, owner_total)

    def for_device(device):
        device_key = jax.random.fold_in(key, device + 1000)
        slot_ids = jax.random.permutation(jax.random.fold_in(device_key, 1), owner_total * CAP)
        slot_owner = slot_ids // CAP
        ranking_key = jnp.where(slot_owner == hot_owner, owner_total * CAP, 0) + jnp.arange(owner_total * CAP)
        ordering = jnp.argsort(ranking_key)
        remaining = slot_ids[ordering[:LAB_DEV - CAP]]
        picked_slots = jnp.concatenate([hot_owner * CAP + jnp.arange(CAP), remaining])
        picked_slots = picked_slots[jax.random.permutation(jax.random.fold_in(device_key, 2), LAB_DEV)]
        inner_leaf = jax.random.randint(jax.random.fold_in(device_key, 3), (LAB_DEV,), 0, LEAF_DEV)
        return picked_slots // CAP * LEAF_DEV + inner_leaf
    return jax.vmap(for_device)(jnp.arange(owner_total)).reshape(-1).astype(jnp.int32)


def set_ends(result, key, least, high):
    place = [jax.random.randint(jax.random.fold_in(key, axis), (), 0, length) for axis, length in enumerate(result.shape)]
    longest = result.shape.index(max(result.shape))
    neighbour = place[:longest] + [(place[longest] + 1) % result.shape[longest]] + place[longest + 1:]
    return result.at[tuple(place)].set(least).at[tuple(neighbour)].set(high)


def shard_levels(rng, shape, split, smallest, high):
    def one(position, blocks):
        draws = jax.random.uniform(jax.random.fold_in(jax.random.fold_in(rng, 6), position), (blocks,), jnp.float32, smallest / len(split), high / len(split))
        return jnp.repeat(jnp.exp(draws), shape[position] // blocks).reshape((-1,) + (1,) * (len(shape) - position - 1))

    gain = one(*split[0])
    for cut in split[1:]:
        gain = gain * one(*cut)
    return gain


def normal_values(key, extent, spread, limit, split=(), dtype=jnp.bfloat16):
    array = jax.random.normal(key, extent, jnp.float32) * spread
    if len(split) > 0:
        array = shard_levels(key, extent, split, -0.22, 0.18) * array
    return jnp.clip(array, min=-limit, max=limit).astype(dtype)


def setup_inputs(seed: int = 0) -> dict:
    arg_keys = jax.random.split(jax.random.key(seed), 8)
    hidden_in = normal_values(arg_keys[0], (LABELS * SEQ, D), 1.0, 6.0, ((0, 8), (1, 4)))
    w_up = normal_values(arg_keys[1], (D, FF), D ** -0.5, 0.21875, ((1, 4),))
    w_down = normal_values(arg_keys[2], (FF, D), FF ** -0.5, 0.109375, ((0, 4),))
    norm_gain = jnp.clip(1.0 + 0.15 * jax.random.normal(arg_keys[3], (D,), jnp.float32), 0.25, 1.75)
    title_length = set_ends(jax.random.randint(arg_keys[4], (LABELS,), 1, SEQ + 1), jax.random.fold_in(arg_keys[4], 1), 1, SEQ).astype(jnp.int32)
    label_leaf = draw_label_leaf(jax.random.fold_in(arg_keys[7], 71), 0)
    leaf_parent = set_ends(jax.random.randint(arg_keys[6], (LEAVES,), 0, PARENTS), jax.random.fold_in(arg_keys[6], 1), 0, PARENTS - 1).astype(jnp.int32)
    return dict(hidden_in=hidden_in, w_up=w_up, w_down=w_down, norm_gain=norm_gain, title_length=title_length, label_leaf=label_leaf, leaf_parent=leaf_parent)


def encode_block(token_block, length_block, w_up, w_down, norm_gain):
    upward = jnp.dot(token_block, w_up, preferred_element_type=jnp.float32)
    activ = jax.nn.gelu(upward, approximate=False).astype(jnp.bfloat16)
    block_units = FF // N_HEADS
    total = jnp.zeros((token_block.shape[0], D), jnp.float32)
    for head_block in range(N_HEADS):
        piece = jnp.dot(activ[:, head_block * block_units:(head_block + 1) * block_units], w_down[head_block * block_units:(head_block + 1) * block_units], preferred_element_type=jnp.float32).astype(jnp.bfloat16)
        piece = lax.optimization_barrier(piece)
        total = total + piece.astype(jnp.float32)
    mixed = (token_block.astype(jnp.float32) + total).astype(jnp.bfloat16)
    mixed = lax.optimization_barrier(mixed)
    as_float = mixed.astype(jnp.float32)
    mean_value = lax.optimization_barrier(jnp.mean(as_float, axis=1, keepdims=True))
    centred = as_float - mean_value
    variance = lax.optimization_barrier(jnp.mean(centred * centred, axis=1, keepdims=True))
    normed = centred * lax.rsqrt(variance + 1e-05) * norm_gain[None, :]
    grouped = normed.reshape(length_block.shape[0], SEQ, D)
    keep_mask = (jnp.arange(SEQ)[None, :] < length_block[:, None]).astype(jnp.float32)
    pooled = lax.optimization_barrier(jnp.sum(grouped * keep_mask[:, :, None], axis=1)) / length_block.astype(jnp.float32)[:, None]
    scale_inv = lax.rsqrt(lax.optimization_barrier(jnp.mean(pooled * pooled, axis=1, keepdims=True)) + 1e-05)
    return (pooled * scale_inv).astype(jnp.bfloat16)

def reference(hidden_in, w_up, w_down, norm_gain, title_length, label_leaf, leaf_parent):
    block_size = math.gcd(LABELS, 256)
    blocks = LABELS // block_size
    token_blocks = hidden_in.reshape(blocks, block_size * SEQ, D)
    length_blocks = title_length.reshape(blocks, block_size)

    def run_block(operand_pair):
        return encode_block(operand_pair[0], operand_pair[1], w_up, w_down, norm_gain)
    label_embed = lax.map(run_block, (token_blocks, length_blocks)).reshape(LABELS, D)
    leaf_sum = jax.ops.segment_sum(label_embed.astype(jnp.float32), label_leaf, num_segments=LEAVES)
    leaf_centers = leaf_sum * lax.rsqrt(lax.optimization_barrier(jnp.mean(leaf_sum * leaf_sum, axis=1, keepdims=True)) + 1e-05)
    parent_sums = jax.ops.segment_sum(leaf_centers, leaf_parent, num_segments=PARENTS)
    return (label_embed, leaf_centers, parent_sums)
```

```python
import functools

import jax
import jax.numpy as jnp
from jax import lax
from jax.experimental import pallas as pl
from jax.experimental.pallas import tpu as pltpu
from jax.sharding import PartitionSpec as P

PAR_DEV = 2
BASE = 128
LANES = 128
UNIT_TILE = 256
VMEM = pl.BlockSpec(memory_space=pltpu.VMEM)
SMEM = pl.BlockSpec(memory_space=pltpu.SMEM)
VMEM_LIMIT = 48 * 1024 * 1024


def call(kernel, out_shape, operands, in_specs, scratch=(), flops=0, bytes_accessed=0):
    return pl.pallas_call(
        kernel,
        out_shape=out_shape,
        in_specs=in_specs,
        out_specs=jax.tree.map(lambda _: VMEM, out_shape),
        scratch_shapes=list(scratch),
        compiler_params=pltpu.CompilerParams(vmem_limit_bytes=VMEM_LIMIT),
        cost_estimate=pl.CostEstimate(
            flops=flops, bytes_accessed=bytes_accessed, transcendentals=0
        ),
    )(*operands)


def split_kernel(place_ref, hidden_ref, mine_ref, other_ref):
    core = place_ref[0] % 2
    quarter = mine_ref.shape[1] // 2
    for pair in range(2):
        to = slice(pair * quarter, (pair + 1) * quarter)
        mine = pl.multiple_of((2 * pair + core) * quarter, quarter)
        other = pl.multiple_of((2 * pair + 1 - core) * quarter, quarter)
        mine_ref[:, to] = hidden_ref[:, pl.ds(mine, quarter)]
        other_ref[:, to] = hidden_ref[:, pl.ds(other, quarter)]


def feed_forward(place_ref, pieces, weights, gathered, own_quarter):
    head = place_ref[0]
    share, both = pieces[0].shape
    quarter = both // 2
    pair = head // 2
    if not own_quarter:
        pair = 1 - pair
    columns = pl.ds(pl.multiple_of(pair * quarter, quarter), quarter)
    for flip, piece in enumerate(pieces):
        source = head ^ flip
        rows = pl.ds(pl.multiple_of(source * share, 64), share)
        gathered[rows, :] = piece[:, columns]
    tokens = gathered[...].T
    total = None
    for up_ref, down_ref in weights:
        units = up_ref.shape[1]
        tile = min(UNIT_TILE, units)
        part = None
        for start in range(0, units, tile):
            upward = jnp.dot(
                tokens, up_ref[:, start : start + tile], preferred_element_type=jnp.float32
            )
            activ = (0.5 * upward * (1.0 + lax.erf(upward * 0.7071067811865476))).astype(
                jnp.bfloat16
            )
            term = jnp.dot(
                activ, down_ref[start : start + tile, :], preferred_element_type=jnp.float32
            )
            part = term if part is None else part + term
        part = part.astype(jnp.bfloat16).astype(jnp.float32)
        total = part if total is None else total + part
    return tokens, total


def give_kernel(place_ref, p0, p1, p2, p3, u0, d0, u1, d1, out_ref, gathered):
    _, total = feed_forward(
        place_ref, (p0, p1, p2, p3), ((u0, d0), (u1, d1)), gathered, own_quarter=False
    )
    out_ref[...] = total.astype(jnp.bfloat16)


def keep_kernel(place_ref, p0, p1, p2, p3, u0, d0, u1, d1, out_ref, gathered):
    tokens, total = feed_forward(
        place_ref, (p0, p1, p2, p3), ((u0, d0), (u1, d1)), gathered, own_quarter=True
    )
    out_ref[...] = tokens.astype(jnp.float32) + total


def embed_kernel(place_ref, length_ref, leaf_ref, parent_ref, kept_ref, came_ref, gain_ref, out_ref):
    head = place_ref[0]
    rows, width = out_ref.shape[0], kept_ref.shape[1]
    seq = kept_ref.shape[0] // rows
    mixed = (kept_ref[...] + came_ref[...].astype(jnp.float32)).astype(jnp.bfloat16)
    as_float = mixed.astype(jnp.float32)
    centred = as_float - jnp.mean(as_float, axis=1, keepdims=True)
    variance = jnp.mean(centred * centred, axis=1, keepdims=True)
    normed = centred * lax.rsqrt(variance + 1e-05) * gain_ref[...]
    position = lax.broadcasted_iota(jnp.int32, (seq, 1), 0)
    row = lax.broadcasted_iota(jnp.int32, (rows, 1), 0)
    lane = lax.broadcasted_iota(jnp.int32, (rows, LANES), 1)
    row_wide = lax.broadcasted_iota(jnp.int32, (rows, LANES), 0)
    pooled = []
    lengths = jnp.ones((rows, 1), jnp.float32)
    indices = jnp.zeros((rows, LANES), jnp.int32)
    for i in range(rows):
        length = length_ref[head * rows + i]
        block = normed[i * seq : (i + 1) * seq]
        pooled.append(
            jnp.sum(jnp.where(position < length, block, 0.0), axis=0, keepdims=True)
        )
        lengths = jnp.where(row == i, length.astype(jnp.float32), lengths)
        leaf = leaf_ref[head * rows + i]
        parent = parent_ref[i]
        for at, digit in enumerate((leaf % BASE, leaf // BASE, parent % BASE, parent // BASE)):
            indices = jnp.where((row_wide == i) & (lane == at), digit, indices)
    pooled = jnp.concatenate(pooled, axis=0) / lengths
    scale = lax.rsqrt(jnp.mean(pooled * pooled, axis=1, keepdims=True) + 1e-05)
    both = jnp.concatenate([pooled * scale, indices.astype(jnp.float32)], axis=1)
    out_ref[...] = both.astype(jnp.bfloat16)


def pick_share(values, head, heads):
    share = values.shape[1] // heads
    result = values[:, :share]
    for other in range(1, heads):
        result = jnp.where(head == other, values[:, other * share : (other + 1) * share], result)
    return result


def leaf_kernel(
    heads, leaf_count, place_ref, near_ref, far_ref, embed_ref, centers_ref, parents_ref, scratch
):
    head, index = place_ref[0], place_ref[1]
    core = head % 2
    width = embed_ref.shape[1]
    rows = embed_ref.shape[0] // heads
    owners = near_ref.shape[0] // (2 * rows)
    leaves = owners * leaf_count
    wanted = lax.broadcasted_iota(jnp.int32, (leaves, near_ref.shape[0]), 0)
    leaf_sum = jnp.zeros((leaves, width), jnp.float32)
    for ref in (near_ref, far_ref):
        digits = ref[:, width:].astype(jnp.float32)
        turned = digits.T
        leaf = (turned[0:1] + BASE * turned[1:2]).astype(jnp.int32)
        picker = jnp.where(wanted == leaf, 1.0, 0.0).astype(jnp.bfloat16)
        leaf_sum = leaf_sum + jnp.dot(
            picker, ref[:, :width], preferred_element_type=jnp.float32
        )
    squares = jnp.mean(leaf_sum * leaf_sum, axis=1, keepdims=True)
    centers = leaf_sum * lax.rsqrt(squares + 1e-05)
    scratch[...] = centers
    own = scratch[pl.ds(pl.multiple_of(index * leaf_count, leaf_count), leaf_count), :]
    centers_ref[...] = pick_share(own, head, heads)
    digits = near_ref[:, width:].astype(jnp.float32)
    digits = digits.reshape(owners, 2, rows, LANES)[:, 0, :leaf_count].reshape(leaves, LANES)
    parent = (digits[:, 2:3] + BASE * digits[:, 3:4]).astype(jnp.int32)
    sums = [
        jnp.sum(jnp.where(parent == index * PAR_DEV + p, centers, 0.0), axis=0, keepdims=True)
        for p in range(PAR_DEV)
    ]
    parents_ref[...] = pick_share(jnp.concatenate(sums, axis=0), head, heads)
    here = pl.ds(pl.multiple_of(index * 2 * rows, 2 * rows), 2 * rows)
    near = near_ref[here, :width].astype(jnp.float32)
    far = far_ref[here, :width].astype(jnp.float32)
    even, odd = jnp.where(core == 0, near, far), jnp.where(core == 0, far, near)
    embed_ref[...] = jnp.concatenate(
        [part[i * rows : (i + 1) * rows] for i in range(2) for part in (even, odd)], axis=0
    ).astype(jnp.bfloat16)


def local(owners, heads, hidden_in, w_up, w_down, norm_gain, title_length, label_leaf, leaf_parent):
    token_rows, share = hidden_in.shape
    width = w_down.shape[1]
    units = w_up.shape[1]
    labels_here = label_leaf.shape[0]
    leaf_count = leaf_parent.shape[0]
    rows = labels_here // heads
    quarter = token_rows // heads
    place = jnp.stack([lax.axis_index("heads"), lax.axis_index("labels")]).astype(jnp.int32)

    def swap(values, flip):
        return lax.ppermute(values, "heads", [(i, i ^ flip) for i in range(heads)])

    up_far, down_far = swap(w_up, 1), swap(w_down, 1)
    half = jax.ShapeDtypeStruct((share, 2 * quarter), jnp.bfloat16)
    mine, other = call(split_kernel, (half, half), (place, hidden_in.T), [SMEM, VMEM])
    pieces = (mine, swap(other, 1), swap(mine, 2), swap(other, 3))
    operands = (place, *pieces, w_up, w_down, up_far, down_far)
    specs = [SMEM] + [VMEM] * 8
    scratch = [pltpu.VMEM((width, quarter), jnp.bfloat16)]
    flops = 8 * quarter * width * units
    given = call(
        give_kernel,
        jax.ShapeDtypeStruct((quarter, width), jnp.bfloat16),
        operands,
        specs,
        scratch,
        flops,
        8 * width * units,
    )
    came = swap(given, 2)
    kept = call(
        keep_kernel,
        jax.ShapeDtypeStruct((quarter, width), jnp.float32),
        operands,
        specs,
        scratch,
        flops,
        8 * width * units,
    )
    message = call(
        embed_kernel,
        jax.ShapeDtypeStruct((rows, width + LANES), jnp.bfloat16),
        (place, title_length, label_leaf, leaf_parent, kept, came, norm_gain[None, :]),
        [SMEM] * 4 + [VMEM] * 3,
    )
    groups = [
        [owner * heads + head for owner in range(owners) for head in range(core, heads, 2)]
        for core in range(2)
    ]
    members = owners * heads // 2
    near = lax.all_to_all(
        jnp.broadcast_to(message[None], (members,) + message.shape),
        ("labels", "heads"),
        split_axis=0,
        concat_axis=0,
        tiled=True,
        axis_index_groups=groups,
    ).reshape(members * rows, width + LANES)
    far = swap(near, 1)
    return call(
        functools.partial(leaf_kernel, heads, leaf_count),
        (
            jax.ShapeDtypeStruct((labels_here, width), jnp.bfloat16),
            jax.ShapeDtypeStruct((leaf_count, share), jnp.float32),
            jax.ShapeDtypeStruct((PAR_DEV, share), jnp.float32),
        ),
        (place, near, far),
        [SMEM, VMEM, VMEM],
        [pltpu.VMEM((owners * leaf_count, width), jnp.float32)],
    )


def solution(mesh):
    in_specs = (
        P("labels", "heads"),
        P(None, "heads"),
        P("heads", None),
        P(),
        P("labels"),
        P("labels"),
        P("labels"),
    )
    out_specs = (P("labels", None), P("labels", "heads"), P("labels", "heads"))
    body = functools.partial(local, mesh.shape["labels"], mesh.shape["heads"])
    return jax.shard_map(body, mesh=mesh, in_specs=in_specs, out_specs=out_specs, check_vma=False)
```

```python
import functools

import jax
import jax.numpy as jnp
from jax import lax
from jax.experimental import pallas as pl
from jax.experimental.pallas import tpu as pltpu
from jax.sharding import PartitionSpec as P

PAR_DEV = 2
BASE = 128
LANES = 128
UNIT_TILE = 256
VMEM = pl.BlockSpec(memory_space=pltpu.VMEM)
HBM = pl.BlockSpec(memory_space=pl.ANY)
VMEM_LIMIT = 40 * 1024 * 1024


def call(kernel, out_shape, operands, out_spec=VMEM, scratch=(), flops=0, moved=0):
    return pl.pallas_call(
        kernel,
        out_shape=out_shape,
        in_specs=[VMEM] * len(operands),
        out_specs=jax.tree.map(lambda _: out_spec, out_shape),
        scratch_shapes=list(scratch),
        compiler_params=pltpu.CompilerParams(vmem_limit_bytes=VMEM_LIMIT),
        cost_estimate=pl.CostEstimate(flops=flops, bytes_accessed=moved, transcendentals=0),
    )(*operands)


def split_kernel(hidden_ref, mine_ref, other_ref):
    core = lax.axis_index("heads") % 2
    quarter = mine_ref.shape[1] // 2
    for pair in range(2):
        to = slice(pair * quarter, (pair + 1) * quarter)
        mine = pl.multiple_of((2 * pair + core) * quarter, quarter)
        other = pl.multiple_of((2 * pair + 1 - core) * quarter, quarter)
        mine_ref[:, to] = hidden_ref[:, pl.ds(mine, quarter)]
        other_ref[:, to] = hidden_ref[:, pl.ds(other, quarter)]


def stage_kernel(up_ref, down_ref, out_ref):
    out_ref[...] = up_ref[:16, :LANES] + down_ref[:16, :LANES]


def feed_forward(pieces, weights, gathered, own_quarter):
    head = lax.axis_index("heads")
    share, both = pieces[0].shape
    quarter = both // 2
    pair = head // 2 if own_quarter else 1 - head // 2
    columns = pl.ds(pl.multiple_of(pair * quarter, quarter), quarter)
    for flip, piece in enumerate(pieces):
        rows = pl.ds(pl.multiple_of((head ^ flip) * share, 64), share)
        gathered[rows, :] = piece[:, columns]
    tokens = gathered[...].T
    total = None
    for up_ref, down_ref in weights:
        units = up_ref.shape[1]
        tile = min(UNIT_TILE, units)
        part = None
        for start in range(0, units, tile):
            upward = jnp.dot(
                tokens, up_ref[:, start : start + tile], preferred_element_type=jnp.float32
            )
            activ = (0.5 * upward * (1.0 + lax.erf(upward * 0.7071067811865476))).astype(
                jnp.bfloat16
            )
            term = jnp.dot(
                activ, down_ref[start : start + tile, :], preferred_element_type=jnp.float32
            )
            part = term if part is None else part + term
        part = part.astype(jnp.bfloat16).astype(jnp.float32)
        total = part if total is None else total + part
    return tokens, total


def give_kernel(p0, p1, p2, p3, u0, d0, u1, d1, staged, out_ref, gathered):
    _, total = feed_forward((p0, p1, p2, p3), ((u0, d0), (u1, d1)), gathered, False)
    out_ref[...] = total.astype(jnp.bfloat16)


def own_column(values_ref, rows, repeat, first):
    shape = (rows * repeat, values_ref.shape[1])
    wanted = first + lax.broadcasted_iota(jnp.int32, shape, 0) // repeat
    lane = lax.broadcasted_iota(jnp.int32, shape, 1)
    values = values_ref[...].astype(jnp.float32)
    return jnp.sum(jnp.where(lane == wanted, values, 0.0), axis=1, keepdims=True)


def keep_kernel(
    p0, p1, p2, p3, u0, d0, u1, d1, length_ref, leaf_ref, parent_ref,
    out_ref, weight_ref, digits_ref, gathered,
):
    head = lax.axis_index("heads")
    rows, lanes = digits_ref.shape
    seq = out_ref.shape[0] // rows
    length = own_column(length_ref, rows, seq, head * rows)
    position = lax.broadcasted_iota(jnp.int32, (rows * seq, 1), 0) % seq
    weight = jnp.where(position.astype(jnp.float32) < length, 1.0 / length, 0.0)
    weight_ref[...] = jnp.broadcast_to(weight, weight_ref.shape)
    lane = lax.broadcasted_iota(jnp.int32, (rows, lanes), 1)
    digits = jnp.zeros((rows, lanes), jnp.int32)
    for at, (ref, first) in enumerate(((leaf_ref, head * rows), (parent_ref, 0))):
        values = own_column(ref, rows, 1, first).astype(jnp.int32)
        digits = jnp.where(lane == 2 * at, values % BASE, digits)
        digits = jnp.where(lane == 2 * at + 1, values // BASE, digits)
    digits_ref[...] = digits.astype(jnp.float32)
    tokens, total = feed_forward((p0, p1, p2, p3), ((u0, d0), (u1, d1)), gathered, True)
    out_ref[...] = tokens.astype(jnp.float32) + total


def embed_kernel(kept_ref, came_ref, weight_ref, digits_ref, gain_ref, out_ref):
    rows, width = digits_ref.shape[0], kept_ref.shape[1]
    mixed = (kept_ref[...] + came_ref[...].astype(jnp.float32)).astype(jnp.bfloat16)
    as_float = mixed.astype(jnp.float32)
    centred = as_float - jnp.mean(as_float, axis=1, keepdims=True)
    variance = jnp.mean(centred * centred, axis=1, keepdims=True)
    weighted = centred * (lax.rsqrt(variance + 1e-05) * weight_ref[:, :1])
    pooled = jnp.sum(weighted.reshape(rows, -1, width), axis=1) * gain_ref[...]
    scale = lax.rsqrt(jnp.mean(pooled * pooled, axis=1, keepdims=True) + 1e-05)
    both = jnp.concatenate([pooled * scale, digits_ref[...]], axis=1)
    out_ref[...] = both.astype(jnp.bfloat16)


def pick_share(values, head, heads):
    share = values.shape[1] // heads
    result = values[:, :share]
    for other in range(1, heads):
        result = jnp.where(head == other, values[:, other * share : (other + 1) * share], result)
    return result


def leaf_kernel(
    heads, near_ref, far_ref, embed_out, centers_out, parents_out,
    embed_ref, centers_ref, parents_ref, scratch, sems,
):
    head, index = lax.axis_index("heads"), lax.axis_index("labels")
    core = head % 2
    width = embed_ref.shape[1]
    rows = embed_ref.shape[0] // heads
    leaf_count = centers_ref.shape[0]
    owners = near_ref.shape[0] // (2 * rows)
    leaves = owners * leaf_count
    here = pl.ds(pl.multiple_of(index * 2 * rows, 2 * rows), 2 * rows)
    near = near_ref[here, :width].astype(jnp.float32)
    far = far_ref[here, :width].astype(jnp.float32)
    even, odd = jnp.where(core == 0, near, far), jnp.where(core == 0, far, near)
    embed_ref[...] = jnp.concatenate(
        [part[i * rows : (i + 1) * rows] for i in range(2) for part in (even, odd)], axis=0
    ).astype(jnp.bfloat16)
    embed_copy = pltpu.make_async_copy(embed_ref, embed_out, sems.at[0])
    embed_copy.start()
    wanted = lax.broadcasted_iota(jnp.int32, (leaves, near_ref.shape[0]), 0)
    leaf_sum = jnp.zeros((leaves, width), jnp.float32)
    for ref in (near_ref, far_ref):
        turned = ref[:, width:].astype(jnp.float32).T
        leaf = (turned[0:1] + BASE * turned[1:2]).astype(jnp.int32)
        picker = jnp.where(wanted == leaf, 1.0, 0.0).astype(jnp.bfloat16)
        leaf_sum = leaf_sum + jnp.dot(
            picker, ref[:, :width], preferred_element_type=jnp.float32
        )
    squares = jnp.mean(leaf_sum * leaf_sum, axis=1, keepdims=True)
    centers = leaf_sum * lax.rsqrt(squares + 1e-05)
    scratch[...] = centers
    own = scratch[pl.ds(pl.multiple_of(index * leaf_count, leaf_count), leaf_count), :]
    centers_ref[...] = pick_share(own, head, heads)
    centers_copy = pltpu.make_async_copy(centers_ref, centers_out, sems.at[1])
    centers_copy.start()
    digits = near_ref[:, width:].astype(jnp.float32)
    digits = digits.reshape(owners, 2, rows, LANES)[:, 0, :leaf_count].reshape(leaves, LANES)
    parent = (digits[:, 2:3] + BASE * digits[:, 3:4]).astype(jnp.int32)
    sums = [
        jnp.sum(jnp.where(parent == index * PAR_DEV + p, centers, 0.0), axis=0, keepdims=True)
        for p in range(PAR_DEV)
    ]
    parents_ref[...] = pick_share(jnp.concatenate(sums, axis=0), head, heads)
    parents_copy = pltpu.make_async_copy(parents_ref, parents_out, sems.at[2])
    parents_copy.start()
    embed_copy.wait()
    centers_copy.wait()
    parents_copy.wait()


def local(owners, heads, hidden_in, w_up, w_down, norm_gain, title_length, label_leaf, leaf_parent):
    token_rows, share = hidden_in.shape
    width = w_down.shape[1]
    units = w_up.shape[1]
    labels_here = label_leaf.shape[0]
    leaf_count = leaf_parent.shape[0]
    rows = labels_here // heads
    quarter = token_rows // heads

    def swap(values, flip):
        return lax.ppermute(values, "heads", [(i, i ^ flip) for i in range(heads)])

    def array(*shape, dtype=jnp.float32):
        return jax.ShapeDtypeStruct(shape, dtype)

    up_far, down_far = swap(w_up, 1), swap(w_down, 1)
    half = array(share, 2 * quarter, dtype=jnp.bfloat16)
    mine, other = call(split_kernel, (half, half), (hidden_in.T,), flops=0)
    pieces = (mine, swap(other, 1), swap(mine, 2), swap(other, 3))
    staged = call(stage_kernel, array(16, LANES, dtype=jnp.bfloat16), (w_up, w_down))
    operands = (*pieces, w_up, w_down, up_far, down_far)
    cost = dict(
        scratch=[pltpu.VMEM((width, quarter), jnp.bfloat16)],
        flops=8 * quarter * width * units,
        moved=8 * width * units,
    )
    given = call(
        give_kernel, array(quarter, width, dtype=jnp.bfloat16), (*operands, staged), **cost
    )
    came = swap(given, 2)
    kept, weight, digits = call(
        keep_kernel,
        (array(quarter, width), array(quarter, LANES), array(rows, LANES)),
        (*operands, title_length[None, :], label_leaf[None, :], leaf_parent[None, :]),
        **cost,
    )
    message = call(
        embed_kernel,
        array(rows, width + LANES, dtype=jnp.bfloat16),
        (kept, came, weight, digits, norm_gain[None, :]),
    )
    groups = [
        [owner * heads + head for owner in range(owners) for head in range(core, heads, 2)]
        for core in range(2)
    ]
    members = owners * heads // 2
    near = lax.all_to_all(
        jnp.broadcast_to(message[None], (members,) + message.shape),
        ("labels", "heads"),
        split_axis=0,
        concat_axis=0,
        tiled=True,
        axis_index_groups=groups,
    ).reshape(members * rows, width + LANES)
    far = swap(near, 1)
    outputs = (
        array(labels_here, width, dtype=jnp.bfloat16),
        array(leaf_count, share),
        array(PAR_DEV, share),
    )
    return call(
        functools.partial(leaf_kernel, heads),
        outputs,
        (near, far),
        out_spec=HBM,
        scratch=[pltpu.VMEM(out.shape, out.dtype) for out in outputs]
        + [pltpu.VMEM((owners * leaf_count, width), jnp.float32), pltpu.SemaphoreType.DMA((3,))],
    )


def solution(mesh):
    in_specs = (
        P("labels", "heads"),
        P(None, "heads"),
        P("heads", None),
        P(),
        P("labels"),
        P("labels"),
        P("labels"),
    )
    out_specs = (P("labels", None), P("labels", "heads"), P("labels", "heads"))
    body = functools.partial(local, mesh.shape["labels"], mesh.shape["heads"])
    return jax.shard_map(body, mesh=mesh, in_specs=in_specs, out_specs=out_specs, check_vma=False)
```

```python
import functools

import jax
import jax.numpy as jnp
from jax import lax
from jax.experimental import pallas as pl
from jax.experimental.pallas import tpu as pltpu
from jax.sharding import PartitionSpec as P

PAR_DEV = 2
BASE = 128
LANES = 128
UNIT_TILE = 768
VMEM = pl.BlockSpec(memory_space=pltpu.VMEM)
HBM = pl.BlockSpec(memory_space=pl.ANY)
VMEM_LIMIT = 40 * 1024 * 1024


def call(kernel, out_shape, operands, out_spec=VMEM, scratch=(), flops=0, moved=0):
    return pl.pallas_call(
        kernel,
        out_shape=out_shape,
        in_specs=[VMEM] * len(operands),
        out_specs=jax.tree.map(lambda _: out_spec, out_shape),
        scratch_shapes=list(scratch),
        compiler_params=pltpu.CompilerParams(vmem_limit_bytes=VMEM_LIMIT),
        cost_estimate=pl.CostEstimate(flops=flops, bytes_accessed=moved, transcendentals=0),
    )(*operands)


def position_kernel(seq, out_ref):
    shape = (out_ref.shape[0], out_ref.shape[1])
    out_ref[...] = (lax.broadcasted_iota(jnp.int32, shape, 0) % seq).astype(jnp.float32)


def merge_kernel(hidden_ref, beside_ref, position_ref, near_ref, far_ref):
    head = lax.axis_index("heads")
    share, quarter = hidden_ref.shape[0], near_ref.shape[1]
    for owner, ref in ((head, near_ref), (head ^ 2, far_ref)):
        columns = pl.ds(pl.multiple_of(owner * quarter, quarter), quarter)
        ref[:share, :] = hidden_ref[:, columns]
        ref[share:, :] = beside_ref[:, columns]


def feed_forward(hidden_ref, beside_ref, across_ref, weights, gathered, owner):
    head = lax.axis_index("heads")
    share, quarter = hidden_ref.shape[0], gathered.shape[1]
    columns = pl.ds(pl.multiple_of(owner * quarter, quarter), quarter)
    pieces = (
        hidden_ref[:, columns],
        beside_ref[:, columns],
        across_ref[:share, :],
        across_ref[share:, :],
    )
    for flip, piece in enumerate(pieces):
        rows = pl.ds(pl.multiple_of((head ^ flip) * share, 64), share)
        gathered[rows, :] = piece
    tokens = gathered[...].T
    total = None
    for up_ref, down_ref in weights:
        units = up_ref.shape[1]
        tile = min(UNIT_TILE, units)
        part = None
        for start in range(0, units, tile):
            upward = jnp.dot(
                tokens, up_ref[:, start : start + tile], preferred_element_type=jnp.float32
            )
            activ = (0.5 * upward * (1.0 + lax.erf(upward * 0.7071067811865476))).astype(
                jnp.bfloat16
            )
            term = jnp.dot(
                activ, down_ref[start : start + tile, :], preferred_element_type=jnp.float32
            )
            part = term if part is None else part + term
        part = part.astype(jnp.bfloat16).astype(jnp.float32)
        total = part if total is None else total + part
    return tokens, total


def give_kernel(hidden_ref, beside_ref, across_ref, u0, d0, u1, d1, out_ref, gathered):
    owner = lax.axis_index("heads") ^ 2
    weights = ((u0, d0), (u1, d1))
    _, total = feed_forward(hidden_ref, beside_ref, across_ref, weights, gathered, owner)
    out_ref[...] = total.astype(jnp.bfloat16)


def own_column(values_ref, rows, repeat, first):
    shape = (rows * repeat, values_ref.shape[1])
    wanted = first + lax.broadcasted_iota(jnp.int32, shape, 0) // repeat
    lane = lax.broadcasted_iota(jnp.int32, shape, 1)
    values = values_ref[...].astype(jnp.float32)
    return jnp.sum(jnp.where(lane == wanted, values, 0.0), axis=1, keepdims=True)


def keep_kernel(
    hidden_ref, beside_ref, across_ref, u0, d0, u1, d1, position_ref, length_ref, leaf_ref, parent_ref,
    out_ref, weight_ref, digits_ref, gathered,
):
    head = lax.axis_index("heads")
    rows, lanes = digits_ref.shape
    seq = out_ref.shape[0] // rows
    length = own_column(length_ref, rows, seq, head * rows)
    weight_ref[...] = jnp.where(position_ref[...] < length, 1.0 / length, 0.0)
    lane = lax.broadcasted_iota(jnp.int32, (rows, lanes), 1)
    digits = jnp.zeros((rows, lanes), jnp.int32)
    for at, (ref, first) in enumerate(
        ((leaf_ref, head * rows), (parent_ref, 0), (leaf_ref, (head ^ 1) * rows))
    ):
        values = own_column(ref, rows, 1, first).astype(jnp.int32)
        digits = jnp.where(lane == 2 * at, values % BASE, digits)
        digits = jnp.where(lane == 2 * at + 1, values // BASE, digits)
    digits_ref[...] = digits.astype(jnp.float32)
    weights = ((u0, d0), (u1, d1))
    tokens, total = feed_forward(hidden_ref, beside_ref, across_ref, weights, gathered, head)
    out_ref[...] = tokens.astype(jnp.float32) + total


def embed_kernel(kept_ref, came_ref, weight_ref, digits_ref, gain_ref, out_ref):
    rows, width = digits_ref.shape[0], kept_ref.shape[1]
    mixed = (kept_ref[...] + came_ref[...].astype(jnp.float32)).astype(jnp.bfloat16)
    as_float = mixed.astype(jnp.float32)
    centred = as_float - jnp.mean(as_float, axis=1, keepdims=True)
    variance = jnp.mean(centred * centred, axis=1, keepdims=True)
    weighted = centred * (lax.rsqrt(variance + 1e-05) * weight_ref[:, :1])
    pooled = jnp.sum(weighted.reshape(rows, -1, width), axis=1) * gain_ref[...]
    scale = lax.rsqrt(jnp.mean(pooled * pooled, axis=1, keepdims=True) + 1e-05)
    both = jnp.concatenate([pooled * scale, digits_ref[...]], axis=1)
    out_ref[...] = both.astype(jnp.bfloat16)


def pick_share(values, head, heads):
    share = values.shape[1] // heads
    result = values[:, :share]
    for other in range(1, heads):
        result = jnp.where(head == other, values[:, other * share : (other + 1) * share], result)
    return result


def near_kernel(leaf_count, near_ref, sum_ref, picker_ref, parent_ref):
    leaves, width = sum_ref.shape
    count = near_ref.shape[0]
    owners = leaves // leaf_count
    digits = near_ref[:, width:].astype(jnp.float32)
    turned = digits.T
    wanted = lax.broadcasted_iota(jnp.int32, (leaves, count), 0)

    def pick(at):
        leaf = (turned[at : at + 1] + BASE * turned[at + 1 : at + 2]).astype(jnp.int32)
        return jnp.where(wanted == leaf, 1.0, 0.0).astype(jnp.bfloat16)

    sum_ref[...] = jnp.dot(pick(0), near_ref[:, :width], preferred_element_type=jnp.float32)
    picker_ref[...] = pick(4)
    digits = digits.reshape(owners, count // owners, LANES)[:, :leaf_count].reshape(leaves, LANES)
    parent = digits[:, 2:3] + BASE * digits[:, 3:4]
    parent_ref[...] = jnp.broadcast_to(parent, parent_ref.shape)


def leaf_kernel(
    heads, near_ref, far_ref, sum_ref, picker_ref, parent_ref,
    embed_out, centers_out, parents_out, embed_ref, centers_ref, parents_ref, scratch, sems,
):
    head, index = lax.axis_index("heads"), lax.axis_index("labels")
    core = head % 2
    width = embed_ref.shape[1]
    rows = embed_ref.shape[0] // heads
    leaf_count = centers_ref.shape[0]
    here = pl.ds(pl.multiple_of(index * 2 * rows, 2 * rows), 2 * rows)
    near = near_ref[here, :width].astype(jnp.float32)
    far = far_ref[here, :width].astype(jnp.float32)
    even, odd = jnp.where(core == 0, near, far), jnp.where(core == 0, far, near)
    embed_ref[...] = jnp.concatenate(
        [part[i * rows : (i + 1) * rows] for i in range(2) for part in (even, odd)], axis=0
    ).astype(jnp.bfloat16)
    embed_copy = pltpu.make_async_copy(embed_ref, embed_out, sems.at[0])
    embed_copy.start()
    leaf_sum = sum_ref[...] + jnp.dot(
        picker_ref[...], far_ref[:, :width], preferred_element_type=jnp.float32
    )
    squares = jnp.mean(leaf_sum * leaf_sum, axis=1, keepdims=True)
    centers = leaf_sum * lax.rsqrt(squares + 1e-05)
    scratch[...] = centers
    own = scratch[pl.ds(pl.multiple_of(index * leaf_count, leaf_count), leaf_count), :]
    centers_ref[...] = pick_share(own, head, heads)
    centers_copy = pltpu.make_async_copy(centers_ref, centers_out, sems.at[1])
    centers_copy.start()
    parent = parent_ref[:, :1].astype(jnp.int32)
    sums = [
        jnp.sum(jnp.where(parent == index * PAR_DEV + p, centers, 0.0), axis=0, keepdims=True)
        for p in range(PAR_DEV)
    ]
    parents_ref[...] = pick_share(jnp.concatenate(sums, axis=0), head, heads)
    parents_copy = pltpu.make_async_copy(parents_ref, parents_out, sems.at[2])
    parents_copy.start()
    embed_copy.wait()
    centers_copy.wait()
    parents_copy.wait()


def local(owners, heads, hidden_in, w_up, w_down, norm_gain, title_length, label_leaf, leaf_parent):
    token_rows, share = hidden_in.shape
    width = w_down.shape[1]
    units = w_up.shape[1]
    labels_here = label_leaf.shape[0]
    leaf_count = leaf_parent.shape[0]
    rows = labels_here // heads
    quarter = token_rows // heads

    def swap(values, flip):
        return lax.ppermute(values, "heads", [(i, i ^ flip) for i in range(heads)])

    def array(*shape, dtype=jnp.float32):
        return jax.ShapeDtypeStruct(shape, dtype)

    hidden = hidden_in.T
    beside = swap(hidden, 1)
    position = call(
        functools.partial(position_kernel, token_rows // labels_here),
        array(quarter, LANES),
        (),
        flops=5000000000,
    )
    merged = array(2 * share, quarter, dtype=jnp.bfloat16)
    near, far = call(merge_kernel, (merged, merged), (hidden, beside, position), flops=10000000000)
    up_far, down_far = swap(w_up, 1), swap(w_down, 1)
    come_give, come_keep = swap(near, 2), swap(far, 2)
    weights = (w_up, w_down, up_far, down_far)
    cost = dict(
        scratch=[pltpu.VMEM((width, quarter), jnp.bfloat16)],
        flops=8 * quarter * width * units,
        moved=8 * width * units,
    )
    given = call(
        give_kernel, array(quarter, width, dtype=jnp.bfloat16), (hidden, beside, come_give, *weights), **cost
    )
    came = swap(given, 2)
    kept, weight, digits = call(
        keep_kernel,
        (array(quarter, width), array(quarter, LANES), array(rows, LANES)),
        (hidden, beside, come_keep, *weights, position, title_length[None, :], label_leaf[None, :], leaf_parent[None, :]),
        **dict(cost, flops=10000000000),
    )
    message = call(
        embed_kernel,
        array(rows, width + LANES, dtype=jnp.bfloat16),
        (kept, came, weight, digits, norm_gain[None, :]),
    )
    groups = [
        [owner * heads + head for owner in range(owners) for head in range(core, heads, 2)]
        for core in range(2)
    ]
    members = owners * heads // 2
    near = lax.all_to_all(
        jnp.broadcast_to(message[None], (members,) + message.shape),
        ("labels", "heads"),
        split_axis=0,
        concat_axis=0,
        tiled=True,
        axis_index_groups=groups,
    ).reshape(members * rows, width + LANES)
    far = swap(near, 1)
    leaves = owners * leaf_count
    ready = call(
        functools.partial(near_kernel, leaf_count),
        (
            array(leaves, width),
            array(leaves, members * rows, dtype=jnp.bfloat16),
            array(leaves, LANES),
        ),
        (near,),
    )
    outputs = (
        array(labels_here, width, dtype=jnp.bfloat16),
        array(leaf_count, share),
        array(PAR_DEV, share),
    )
    return call(
        functools.partial(leaf_kernel, heads),
        outputs,
        (near, far, *ready),
        out_spec=HBM,
        scratch=[pltpu.VMEM(out.shape, out.dtype) for out in outputs]
        + [pltpu.VMEM((leaves, width), jnp.float32), pltpu.SemaphoreType.DMA((3,))],
    )


def solution(mesh):
    in_specs = (
        P("labels", "heads"),
        P(None, "heads"),
        P("heads", None),
        P(),
        P("labels"),
        P("labels"),
        P("labels"),
    )
    out_specs = (P("labels", None), P("labels", "heads"), P("labels", "heads"))
    body = functools.partial(local, mesh.shape["labels"], mesh.shape["heads"])
    return jax.shard_map(body, mesh=mesh, in_specs=in_specs, out_specs=out_specs, check_vma=False)
```

```python
import functools

import jax
import jax.numpy as jnp
from jax import lax
from jax.experimental import pallas as pl
from jax.experimental.pallas import tpu as pltpu
from jax.sharding import PartitionSpec as P

PAR_DEV = 2
BASE = 128
LANES = 128
UNIT_TILE = 768
VMEM = pl.BlockSpec(memory_space=pltpu.VMEM)
HBM = pl.BlockSpec(memory_space=pl.ANY)
VMEM_LIMIT = 40 * 1024 * 1024


def call(kernel, out_shape, operands, out_spec=VMEM, scratch=(), flops=0, moved=0):
    return pl.pallas_call(
        kernel,
        out_shape=out_shape,
        in_specs=[VMEM] * len(operands),
        out_specs=jax.tree.map(lambda _: out_spec, out_shape),
        scratch_shapes=list(scratch),
        compiler_params=pltpu.CompilerParams(vmem_limit_bytes=VMEM_LIMIT),
        cost_estimate=pl.CostEstimate(flops=flops, bytes_accessed=moved, transcendentals=0),
    )(*operands)


def position_kernel(seq, out_ref):
    shape = (out_ref.shape[0], out_ref.shape[1])
    out_ref[...] = (lax.broadcasted_iota(jnp.int32, shape, 0) % seq).astype(jnp.float32)


def merge_kernel(hidden_ref, beside_ref, position_ref, near_ref, far_ref):
    head = lax.axis_index("heads")
    share, quarter = hidden_ref.shape[0], near_ref.shape[1]
    for owner, ref in ((head, near_ref), (head ^ 2, far_ref)):
        columns = pl.ds(pl.multiple_of(owner * quarter, quarter), quarter)
        ref[:share, :] = hidden_ref[:, columns]
        ref[share:, :] = beside_ref[:, columns]


def feed_forward(hidden_ref, beside_ref, across_ref, weights, gathered, owner):
    head = lax.axis_index("heads")
    share, quarter = hidden_ref.shape[0], gathered.shape[1]
    columns = pl.ds(pl.multiple_of(owner * quarter, quarter), quarter)
    pieces = (
        hidden_ref[:, columns],
        beside_ref[:, columns],
        across_ref[:share, :],
        across_ref[share:, :],
    )
    for flip, piece in enumerate(pieces):
        rows = pl.ds(pl.multiple_of((head ^ flip) * share, 64), share)
        gathered[rows, :] = piece
    tokens = gathered[...].T
    total = None
    for up_ref, down_ref in weights:
        units = up_ref.shape[1]
        tile = min(UNIT_TILE, units)
        part = None
        for start in range(0, units, tile):
            upward = jnp.dot(
                tokens, up_ref[:, start : start + tile], preferred_element_type=jnp.float32
            )
            activ = (0.5 * upward * (1.0 + lax.erf(upward * 0.7071067811865476))).astype(
                jnp.bfloat16
            )
            term = jnp.dot(
                activ, down_ref[start : start + tile, :], preferred_element_type=jnp.float32
            )
            part = term if part is None else part + term
        part = part.astype(jnp.bfloat16).astype(jnp.float32)
        total = part if total is None else total + part
    return tokens, total


def give_kernel(hidden_ref, beside_ref, across_ref, u0, d0, u1, d1, out_ref, gathered):
    owner = lax.axis_index("heads") ^ 2
    weights = ((u0, d0), (u1, d1))
    _, total = feed_forward(hidden_ref, beside_ref, across_ref, weights, gathered, owner)
    out_ref[...] = total.astype(jnp.bfloat16)


def own_column(values_ref, rows, repeat, first):
    shape = (rows * repeat, values_ref.shape[1])
    wanted = first + lax.broadcasted_iota(jnp.int32, shape, 0) // repeat
    lane = lax.broadcasted_iota(jnp.int32, shape, 1)
    values = values_ref[...].astype(jnp.float32)
    return jnp.sum(jnp.where(lane == wanted, values, 0.0), axis=1, keepdims=True)


def keep_kernel(
    hidden_ref, beside_ref, across_ref, u0, d0, u1, d1, position_ref, length_ref, leaf_ref, parent_ref,
    out_ref, weight_ref, digits_ref, gathered,
):
    head = lax.axis_index("heads")
    rows, lanes = digits_ref.shape
    seq = out_ref.shape[0] // rows
    length = own_column(length_ref, rows, seq, head * rows)
    weight_ref[...] = jnp.where(position_ref[...] < length, 1.0 / length, 0.0)
    lane = lax.broadcasted_iota(jnp.int32, (rows, lanes), 1)
    digits = jnp.zeros((rows, lanes), jnp.int32)
    for at, (ref, first) in enumerate(
        ((leaf_ref, head * rows), (parent_ref, 0), (leaf_ref, (head ^ 1) * rows))
    ):
        values = own_column(ref, rows, 1, first).astype(jnp.int32)
        digits = jnp.where(lane == 2 * at, values % BASE, digits)
        digits = jnp.where(lane == 2 * at + 1, values // BASE, digits)
    digits_ref[...] = digits.astype(jnp.float32)
    weights = ((u0, d0), (u1, d1))
    tokens, total = feed_forward(hidden_ref, beside_ref, across_ref, weights, gathered, head)
    out_ref[...] = tokens.astype(jnp.float32) + total


def embed_kernel(kept_ref, came_ref, weight_ref, digits_ref, gain_ref, out_ref):
    rows, width = digits_ref.shape[0], kept_ref.shape[1]
    mixed = (kept_ref[...] + came_ref[...].astype(jnp.float32)).astype(jnp.bfloat16)
    as_float = mixed.astype(jnp.float32)
    centred = as_float - jnp.mean(as_float, axis=1, keepdims=True)
    variance = jnp.mean(centred * centred, axis=1, keepdims=True)
    weighted = centred * (lax.rsqrt(variance + 1e-05) * weight_ref[:, :1])
    pooled = jnp.sum(weighted.reshape(rows, -1, width), axis=1) * gain_ref[...]
    scale = lax.rsqrt(jnp.mean(pooled * pooled, axis=1, keepdims=True) + 1e-05)
    both = jnp.concatenate([pooled * scale, digits_ref[...]], axis=1)
    out_ref[...] = both.astype(jnp.bfloat16)


def pick_share(values, head, heads):
    share = values.shape[1] // heads
    result = values[:, :share]
    for other in range(1, heads):
        result = jnp.where(head == other, values[:, other * share : (other + 1) * share], result)
    return result


def position_of(owners, owner):
    half = owners // 2
    return (1 - owner % 2) * half + half - 1 - owner // 2


def owner_at(owners, position):
    half = owners // 2
    odd = jnp.where(position < half, 1, 0)
    return 2 * (half - 1 - position + (1 - odd) * half) + odd


def near_kernel(leaf_count, near_ref, sum_ref, picker_ref, parent_ref):
    leaves, width = sum_ref.shape
    count = near_ref.shape[0]
    owners = leaves // leaf_count
    digits = near_ref[:, width:].astype(jnp.float32)
    turned = digits.T
    row = lax.broadcasted_iota(jnp.int32, (leaves, count), 0)
    wanted = owner_at(owners, row // leaf_count) * leaf_count + row % leaf_count

    def pick(at):
        leaf = (turned[at : at + 1] + BASE * turned[at + 1 : at + 2]).astype(jnp.int32)
        return jnp.where(wanted == leaf, 1.0, 0.0).astype(jnp.bfloat16)

    sum_ref[...] = jnp.dot(pick(0), near_ref[:, :width], preferred_element_type=jnp.float32)
    picker_ref[...] = pick(4)
    digits = digits.reshape(owners, count // owners, LANES)[:, :leaf_count].reshape(leaves, LANES)
    parent = digits[:, 2:3] + BASE * digits[:, 3:4]
    parent_ref[...] = jnp.broadcast_to(parent, parent_ref.shape)


def leaf_kernel(
    heads, near_ref, far_ref, sum_ref, picker_ref, parent_ref,
    embed_out, centers_out, parents_out, embed_ref, centers_ref, parents_ref, scratch, sems,
):
    head, index = lax.axis_index("heads"), lax.axis_index("labels")
    core = head % 2
    width = embed_ref.shape[1]
    rows = embed_ref.shape[0] // heads
    leaf_count = centers_ref.shape[0]
    position = position_of(sum_ref.shape[0] // leaf_count, index)
    here = pl.ds(pl.multiple_of(position * 2 * rows, 2 * rows), 2 * rows)
    near = near_ref[here, :width].astype(jnp.float32)
    far = far_ref[here, :width].astype(jnp.float32)
    even, odd = jnp.where(core == 0, near, far), jnp.where(core == 0, far, near)
    embed_ref[...] = jnp.concatenate(
        [part[i * rows : (i + 1) * rows] for i in (1, 0) for part in (even, odd)], axis=0
    ).astype(jnp.bfloat16)
    embed_copy = pltpu.make_async_copy(embed_ref, embed_out, sems.at[0])
    embed_copy.start()
    leaf_sum = sum_ref[...] + jnp.dot(
        picker_ref[...], far_ref[:, :width], preferred_element_type=jnp.float32
    )
    squares = jnp.mean(leaf_sum * leaf_sum, axis=1, keepdims=True)
    centers = leaf_sum * lax.rsqrt(squares + 1e-05)
    scratch[...] = centers
    own = scratch[pl.ds(pl.multiple_of(position * leaf_count, leaf_count), leaf_count), :]
    centers_ref[...] = pick_share(own, head, heads)
    centers_copy = pltpu.make_async_copy(centers_ref, centers_out, sems.at[1])
    centers_copy.start()
    parent = parent_ref[:, :1].astype(jnp.int32)
    sums = [
        jnp.sum(jnp.where(parent == index * PAR_DEV + p, centers, 0.0), axis=0, keepdims=True)
        for p in range(PAR_DEV)
    ]
    parents_ref[...] = pick_share(jnp.concatenate(sums, axis=0), head, heads)
    parents_copy = pltpu.make_async_copy(parents_ref, parents_out, sems.at[2])
    parents_copy.start()
    embed_copy.wait()
    centers_copy.wait()
    parents_copy.wait()


def local(owners, heads, hidden_in, w_up, w_down, norm_gain, title_length, label_leaf, leaf_parent):
    token_rows, share = hidden_in.shape
    width = w_down.shape[1]
    units = w_up.shape[1]
    labels_here = label_leaf.shape[0]
    leaf_count = leaf_parent.shape[0]
    rows = labels_here // heads
    quarter = token_rows // heads

    def swap(values, flip):
        return lax.ppermute(values, "heads", [(i, i ^ flip) for i in range(heads)])

    def array(*shape, dtype=jnp.float32):
        return jax.ShapeDtypeStruct(shape, dtype)

    hidden = hidden_in.T
    beside = swap(hidden, 1)
    position = call(
        functools.partial(position_kernel, token_rows // labels_here),
        array(quarter, LANES),
        (),
        flops=5000000000,
    )
    merged = array(2 * share, quarter, dtype=jnp.bfloat16)
    near, far = call(merge_kernel, (merged, merged), (hidden, beside, position), flops=10000000000)
    up_far, down_far = swap(w_up, 1), swap(w_down, 1)
    come_give, come_keep = swap(near, 2), swap(far, 2)
    weights = (w_up, w_down, up_far, down_far)
    cost = dict(
        scratch=[pltpu.VMEM((width, quarter), jnp.bfloat16)],
        flops=8 * quarter * width * units,
        moved=8 * width * units,
    )
    given = call(
        give_kernel, array(quarter, width, dtype=jnp.bfloat16), (hidden, beside, come_give, *weights), **cost
    )
    came = swap(given, 2)
    kept, weight, digits = call(
        keep_kernel,
        (array(quarter, width), array(quarter, LANES), array(rows, LANES)),
        (hidden, beside, come_keep, *weights, position, title_length[None, :], label_leaf[None, :], leaf_parent[None, :]),
        **dict(cost, flops=10000000000),
    )
    message = call(
        embed_kernel,
        array(rows, width + LANES, dtype=jnp.bfloat16),
        (kept, came, weight, digits, norm_gain[None, :]),
    )
    groups = [
        [
            owner * heads + head
            for owner in sorted(range(owners), key=functools.partial(position_of, owners))
            for head in reversed(range(core, heads, 2))
        ]
        for core in range(2)
    ]
    members = owners * heads // 2
    near = lax.all_to_all(
        jnp.broadcast_to(message[None], (members,) + message.shape),
        ("labels", "heads"),
        split_axis=0,
        concat_axis=0,
        tiled=True,
        axis_index_groups=groups,
    ).reshape(members * rows, width + LANES)
    far = swap(near, 1)
    leaves = owners * leaf_count
    ready = call(
        functools.partial(near_kernel, leaf_count),
        (
            array(leaves, width),
            array(leaves, members * rows, dtype=jnp.bfloat16),
            array(leaves, LANES),
        ),
        (near,),
    )
    outputs = (
        array(labels_here, width, dtype=jnp.bfloat16),
        array(leaf_count, share),
        array(PAR_DEV, share),
    )
    return call(
        functools.partial(leaf_kernel, heads),
        outputs,
        (near, far, *ready),
        out_spec=HBM,
        scratch=[pltpu.VMEM(out.shape, out.dtype) for out in outputs]
        + [pltpu.VMEM((leaves, width), jnp.float32), pltpu.SemaphoreType.DMA((3,))],
    )


def solution(mesh):
    in_specs = (
        P("labels", "heads"),
        P(None, "heads"),
        P("heads", None),
        P(),
        P("labels"),
        P("labels"),
        P("labels"),
    )
    out_specs = (P("labels", None), P("labels", "heads"), P("labels", "heads"))
    body = functools.partial(local, mesh.shape["labels"], mesh.shape["heads"])
    return jax.shard_map(body, mesh=mesh, in_specs=in_specs, out_specs=out_specs, check_vma=False)
```

```python
import functools

import jax
import jax.numpy as jnp
from jax import lax
from jax.experimental import pallas as pl
from jax.experimental.pallas import tpu as pltpu
from jax.sharding import PartitionSpec as P

PAR_DEV = 2
BASE = 128
LANES = 128
UNIT_TILE = 768
VMEM = pl.BlockSpec(memory_space=pltpu.VMEM)
HBM = pl.BlockSpec(memory_space=pl.ANY)
VMEM_LIMIT = 40 * 1024 * 1024


def call(kernel, out_shape, operands, out_spec=VMEM, scratch=(), flops=0, moved=0):
    return pl.pallas_call(
        kernel,
        out_shape=out_shape,
        in_specs=[VMEM] * len(operands),
        out_specs=jax.tree.map(lambda _: out_spec, out_shape),
        scratch_shapes=list(scratch),
        compiler_params=pltpu.CompilerParams(vmem_limit_bytes=VMEM_LIMIT),
        cost_estimate=pl.CostEstimate(flops=flops, bytes_accessed=moved, transcendentals=0),
    )(*operands)


def position_kernel(seq, out_ref):
    shape = (out_ref.shape[0], out_ref.shape[1])
    out_ref[...] = (lax.broadcasted_iota(jnp.int32, shape, 0) % seq).astype(jnp.float32)


def quarter_of(ref, owner, quarter):
    return ref[:, pl.ds(pl.multiple_of(owner * quarter, quarter), quarter)]


def own_kernel(hidden_ref, position_ref, near_ref):
    near_ref[...] = quarter_of(hidden_ref, lax.axis_index("heads"), near_ref.shape[1])


def merge_kernel(hidden_ref, beside_ref, near_ref, far_ref):
    head = lax.axis_index("heads")
    share, quarter = near_ref.shape
    near_ref[...] = quarter_of(beside_ref, head, quarter)
    far_ref[:share, :] = quarter_of(hidden_ref, head ^ 2, quarter)
    far_ref[share:, :] = quarter_of(beside_ref, head ^ 2, quarter)


def feed_forward(hidden_ref, beside_ref, across, weights, gathered, owner):
    head = lax.axis_index("heads")
    share, quarter = hidden_ref.shape[0], gathered.shape[1]
    pieces = (
        quarter_of(hidden_ref, owner, quarter),
        quarter_of(beside_ref, owner, quarter),
        *across,
    )
    for flip, piece in enumerate(pieces):
        rows = pl.ds(pl.multiple_of((head ^ flip) * share, 64), share)
        gathered[rows, :] = piece
    tokens = gathered[...].T
    total = None
    for up_ref, down_ref in weights:
        units = up_ref.shape[1]
        tile = min(UNIT_TILE, units)
        part = None
        for start in range(0, units, tile):
            upward = jnp.dot(
                tokens, up_ref[:, start : start + tile], preferred_element_type=jnp.float32
            )
            activ = (0.5 * upward * (1.0 + lax.erf(upward * 0.7071067811865476))).astype(
                jnp.bfloat16
            )
            term = jnp.dot(
                activ, down_ref[start : start + tile, :], preferred_element_type=jnp.float32
            )
            part = term if part is None else part + term
        part = part.astype(jnp.bfloat16).astype(jnp.float32)
        total = part if total is None else total + part
    return tokens, total


def give_kernel(hidden_ref, beside_ref, across_ref, diagonal_ref, u0, d0, u1, d1, out_ref, gathered):
    owner = lax.axis_index("heads") ^ 2
    weights = ((u0, d0), (u1, d1))
    across = (across_ref[...], diagonal_ref[...])
    _, total = feed_forward(hidden_ref, beside_ref, across, weights, gathered, owner)
    out_ref[...] = total.astype(jnp.bfloat16)


def own_column(values_ref, rows, repeat, first):
    shape = (rows * repeat, values_ref.shape[1])
    wanted = first + lax.broadcasted_iota(jnp.int32, shape, 0) // repeat
    lane = lax.broadcasted_iota(jnp.int32, shape, 1)
    values = values_ref[...].astype(jnp.float32)
    return jnp.sum(jnp.where(lane == wanted, values, 0.0), axis=1, keepdims=True)


def keep_kernel(
    hidden_ref, beside_ref, across_ref, u0, d0, u1, d1, position_ref, length_ref, leaf_ref, parent_ref,
    out_ref, weight_ref, digits_ref, gathered,
):
    head = lax.axis_index("heads")
    rows, lanes = digits_ref.shape
    seq = out_ref.shape[0] // rows
    length = own_column(length_ref, rows, seq, head * rows)
    weight_ref[...] = jnp.where(position_ref[...] < length, 1.0 / length, 0.0)
    lane = lax.broadcasted_iota(jnp.int32, (rows, lanes), 1)
    digits = jnp.zeros((rows, lanes), jnp.int32)
    for at, (ref, first) in enumerate(
        ((leaf_ref, head * rows), (parent_ref, 0), (leaf_ref, (head ^ 1) * rows))
    ):
        values = own_column(ref, rows, 1, first).astype(jnp.int32)
        digits = jnp.where(lane == 2 * at, values % BASE, digits)
        digits = jnp.where(lane == 2 * at + 1, values // BASE, digits)
    digits_ref[...] = digits.astype(jnp.float32)
    weights = ((u0, d0), (u1, d1))
    share = hidden_ref.shape[0]
    across = (across_ref[:share, :], across_ref[share:, :])
    tokens, total = feed_forward(hidden_ref, beside_ref, across, weights, gathered, head)
    out_ref[...] = tokens.astype(jnp.float32) + total


def embed_kernel(kept_ref, came_ref, weight_ref, digits_ref, gain_ref, out_ref):
    rows, width = digits_ref.shape[0], kept_ref.shape[1]
    mixed = (kept_ref[...] + came_ref[...].astype(jnp.float32)).astype(jnp.bfloat16)
    as_float = mixed.astype(jnp.float32)
    centred = as_float - jnp.mean(as_float, axis=1, keepdims=True)
    variance = jnp.mean(centred * centred, axis=1, keepdims=True)
    weighted = centred * (lax.rsqrt(variance + 1e-05) * weight_ref[:, :1])
    pooled = jnp.sum(weighted.reshape(rows, -1, width), axis=1) * gain_ref[...]
    scale = lax.rsqrt(jnp.mean(pooled * pooled, axis=1, keepdims=True) + 1e-05)
    both = jnp.concatenate([pooled * scale, digits_ref[...]], axis=1)
    out_ref[...] = both.astype(jnp.bfloat16)


def pick_share(values, head, heads):
    share = values.shape[1] // heads
    result = values[:, :share]
    for other in range(1, heads):
        result = jnp.where(head == other, values[:, other * share : (other + 1) * share], result)
    return result


def position_of(owners, owner):
    half = owners // 2
    return (1 - owner % 2) * half + half - 1 - owner // 2


def owner_at(owners, position):
    half = owners // 2
    odd = jnp.where(position < half, 1, 0)
    return 2 * (half - 1 - position + (1 - odd) * half) + odd


def near_kernel(heads, leaf_count, near_ref, sum_ref, share_ref, picker_ref, parent_ref):
    leaves, width = sum_ref.shape
    count = near_ref.shape[0]
    owners = leaves // leaf_count
    digits = near_ref[:, width:].astype(jnp.float32)
    turned = digits.T
    row = lax.broadcasted_iota(jnp.int32, (leaves, count), 0)
    wanted = owner_at(owners, row // leaf_count) * leaf_count + row % leaf_count

    def pick(at):
        leaf = (turned[at : at + 1] + BASE * turned[at + 1 : at + 2]).astype(jnp.int32)
        return jnp.where(wanted == leaf, 1.0, 0.0).astype(jnp.bfloat16)

    near_sum = jnp.dot(pick(0), near_ref[:, :width], preferred_element_type=jnp.float32)
    sum_ref[...] = near_sum
    share_ref[...] = pick_share(near_sum, lax.axis_index("heads"), heads)
    picker_ref[...] = pick(4)
    digits = digits.reshape(owners, count // owners, LANES)[:, :leaf_count].reshape(leaves, LANES)
    parent = digits[:, 2:3] + BASE * digits[:, 3:4]
    parent_ref[...] = jnp.broadcast_to(parent, parent_ref.shape)


def leaf_kernel(
    heads, near_ref, far_ref, sum_ref, share_ref, picker_ref, parent_ref,
    embed_out, centers_out, parents_out, embed_ref, centers_ref, parents_ref, scratch, sems,
):
    head, index = lax.axis_index("heads"), lax.axis_index("labels")
    core = head % 2
    width = embed_ref.shape[1]
    rows = embed_ref.shape[0] // heads
    leaf_count = centers_ref.shape[0]
    position = position_of(sum_ref.shape[0] // leaf_count, index)
    here = pl.ds(pl.multiple_of(position * 2 * rows, 2 * rows), 2 * rows)
    near = near_ref[here, :width].astype(jnp.float32)
    far = far_ref[here, :width].astype(jnp.float32)
    even, odd = jnp.where(core == 0, near, far), jnp.where(core == 0, far, near)
    embed_ref[...] = jnp.concatenate(
        [part[i * rows : (i + 1) * rows] for i in (1, 0) for part in (even, odd)], axis=0
    ).astype(jnp.bfloat16)
    embed_copy = pltpu.make_async_copy(embed_ref, embed_out, sems.at[0])
    embed_copy.start()
    picker = picker_ref[...]
    leaf_sum = sum_ref[...] + jnp.dot(
        picker, far_ref[:, :width], preferred_element_type=jnp.float32
    )
    far_share = pick_share(far_ref[:, :width], head, heads)
    leaf_share = share_ref[...] + jnp.dot(picker, far_share, preferred_element_type=jnp.float32)
    squares = jnp.mean(leaf_sum * leaf_sum, axis=1, keepdims=True)
    centers = leaf_share * lax.rsqrt(squares + 1e-05)
    scratch[...] = centers
    centers_ref[...] = scratch[pl.ds(pl.multiple_of(position * leaf_count, leaf_count), leaf_count), :]
    centers_copy = pltpu.make_async_copy(centers_ref, centers_out, sems.at[1])
    centers_copy.start()
    parent = parent_ref[:, :1].astype(jnp.int32)
    sums = [
        jnp.sum(jnp.where(parent == index * PAR_DEV + p, centers, 0.0), axis=0, keepdims=True)
        for p in range(PAR_DEV)
    ]
    parents_ref[...] = jnp.concatenate(sums, axis=0)
    parents_copy = pltpu.make_async_copy(parents_ref, parents_out, sems.at[2])
    parents_copy.start()
    embed_copy.wait()
    centers_copy.wait()
    parents_copy.wait()


def local(owners, heads, hidden_in, w_up, w_down, norm_gain, title_length, label_leaf, leaf_parent):
    token_rows, share = hidden_in.shape
    width = w_down.shape[1]
    units = w_up.shape[1]
    labels_here = label_leaf.shape[0]
    leaf_count = leaf_parent.shape[0]
    rows = labels_here // heads
    quarter = token_rows // heads

    def swap(values, flip):
        return lax.ppermute(values, "heads", [(i, i ^ flip) for i in range(heads)])

    def array(*shape, dtype=jnp.float32):
        return jax.ShapeDtypeStruct(shape, dtype)

    hidden = hidden_in.T
    beside = swap(hidden, 1)
    position = call(
        functools.partial(position_kernel, token_rows // labels_here),
        array(quarter, LANES),
        (),
        flops=5000000000,
    )
    up_far, down_far = swap(w_up, 1), swap(w_down, 1)
    piece = array(share, quarter, dtype=jnp.bfloat16)
    across = swap(call(own_kernel, piece, (hidden, position), flops=5000000000), 2)
    near, far = call(
        merge_kernel,
        (piece, array(2 * share, quarter, dtype=jnp.bfloat16)),
        (hidden, beside),
        flops=10000000000,
    )
    diagonal = swap(near, 2)
    come_keep = swap(far, 2)
    weights = (w_up, w_down, up_far, down_far)
    cost = dict(
        scratch=[pltpu.VMEM((width, quarter), jnp.bfloat16)],
        flops=8 * quarter * width * units,
        moved=8 * width * units,
    )
    given = call(
        give_kernel, array(quarter, width, dtype=jnp.bfloat16), (hidden, beside, across, diagonal, *weights), **cost
    )
    came = swap(given, 2)
    kept, weight, digits = call(
        keep_kernel,
        (array(quarter, width), array(quarter, LANES), array(rows, LANES)),
        (hidden, beside, come_keep, *weights, position, title_length[None, :], label_leaf[None, :], leaf_parent[None, :]),
        **dict(cost, flops=10000000000),
    )
    message = call(
        embed_kernel,
        array(rows, width + LANES, dtype=jnp.bfloat16),
        (kept, came, weight, digits, norm_gain[None, :]),
    )
    groups = [
        [
            owner * heads + head
            for owner in sorted(range(owners), key=functools.partial(position_of, owners))
            for head in reversed(range(core, heads, 2))
        ]
        for core in range(2)
    ]
    members = owners * heads // 2
    near = lax.all_to_all(
        jnp.broadcast_to(message[None], (members,) + message.shape),
        ("labels", "heads"),
        split_axis=0,
        concat_axis=0,
        tiled=True,
        axis_index_groups=groups,
    ).reshape(members * rows, width + LANES)
    far = swap(near, 1)
    leaves = owners * leaf_count
    ready = call(
        functools.partial(near_kernel, heads, leaf_count),
        (
            array(leaves, width),
            array(leaves, share),
            array(leaves, members * rows, dtype=jnp.bfloat16),
            array(leaves, LANES),
        ),
        (near,),
    )
    outputs = (
        array(labels_here, width, dtype=jnp.bfloat16),
        array(leaf_count, share),
        array(PAR_DEV, share),
    )
    return call(
        functools.partial(leaf_kernel, heads),
        outputs,
        (near, far, *ready),
        out_spec=HBM,
        scratch=[pltpu.VMEM(out.shape, out.dtype) for out in outputs]
        + [pltpu.VMEM((leaves, share), jnp.float32), pltpu.SemaphoreType.DMA((3,))],
    )


def solution(mesh):
    in_specs = (
        P("labels", "heads"),
        P(None, "heads"),
        P("heads", None),
        P(),
        P("labels"),
        P("labels"),
        P("labels"),
    )
    out_specs = (P("labels", None), P("labels", "heads"), P("labels", "heads"))
    body = functools.partial(local, mesh.shape["labels"], mesh.shape["heads"])
    return jax.shard_map(body, mesh=mesh, in_specs=in_specs, out_specs=out_specs, check_vma=False)
```

```python
import functools

import jax
import jax.numpy as jnp
from jax import lax
from jax.experimental import pallas as pl
from jax.experimental.pallas import tpu as pltpu
from jax.sharding import PartitionSpec as P

PAR_DEV = 2
STRIDE = 5
BASE = 128
LANES = 128
UNIT_TILE = 768
VMEM = pl.BlockSpec(memory_space=pltpu.VMEM)
HBM = pl.BlockSpec(memory_space=pl.ANY)
VMEM_LIMIT = 40 * 1024 * 1024


def call(kernel, out_shape, operands, out_spec=VMEM, scratch=(), flops=0, moved=0):
    return pl.pallas_call(
        kernel,
        out_shape=out_shape,
        in_specs=[VMEM] * len(operands),
        out_specs=jax.tree.map(lambda _: out_spec, out_shape),
        scratch_shapes=list(scratch),
        compiler_params=pltpu.CompilerParams(vmem_limit_bytes=VMEM_LIMIT),
        cost_estimate=pl.CostEstimate(flops=flops, bytes_accessed=moved, transcendentals=0),
    )(*operands)


def position_kernel(seq, out_ref):
    shape = (out_ref.shape[0], out_ref.shape[1])
    out_ref[...] = (lax.broadcasted_iota(jnp.int32, shape, 0) % seq).astype(jnp.float32)


def quarter_of(ref, owner, quarter):
    return ref[:, pl.ds(pl.multiple_of(owner * quarter, quarter), quarter)]


def own_kernel(hidden_ref, position_ref, near_ref):
    near_ref[...] = quarter_of(hidden_ref, lax.axis_index("heads"), near_ref.shape[1])


def merge_kernel(hidden_ref, beside_ref, near_ref, far_ref):
    head = lax.axis_index("heads")
    share, quarter = near_ref.shape
    near_ref[...] = quarter_of(beside_ref, head, quarter)
    far_ref[:share, :] = quarter_of(hidden_ref, head ^ 2, quarter)
    far_ref[share:, :] = quarter_of(beside_ref, head ^ 2, quarter)


def gelu(upward):
    return (0.5 * upward * (1.0 + lax.erf(upward * 0.7071067811865476))).astype(jnp.bfloat16)


def feed_forward(hidden_ref, beside_ref, across, weights, gathered, owner):
    head = lax.axis_index("heads")
    share, quarter = hidden_ref.shape[0], gathered.shape[1]
    pieces = (
        quarter_of(hidden_ref, owner, quarter),
        quarter_of(beside_ref, owner, quarter),
        *across,
    )
    for flip, piece in enumerate(pieces):
        rows = pl.ds(pl.multiple_of((head ^ flip) * share, 64), share)
        gathered[rows, :] = piece
    tokens = gathered[...].T
    total = None
    for up_ref, down_ref in weights:
        units = up_ref.shape[1]
        tile = min(UNIT_TILE, units)
        part = None
        for start in range(0, units, tile):
            upward = jnp.dot(
                tokens, up_ref[:, start : start + tile], preferred_element_type=jnp.float32
            )
            term = jnp.dot(
                gelu(upward),
                down_ref[start : start + tile, :],
                preferred_element_type=jnp.float32,
            )
            part = term if part is None else part + term
        part = part.astype(jnp.bfloat16).astype(jnp.float32)
        total = part if total is None else total + part
    return tokens, total


def pair_tokens(near_ref, other_ref, columns, gathered):
    head = lax.axis_index("heads")
    share = near_ref.shape[0]
    gathered[pl.ds(pl.multiple_of(head % 2 * share, 64), share), :] = near_ref[:, columns]
    gathered[pl.ds(pl.multiple_of((head + 1) % 2 * share, 64), share), :] = other_ref[:, columns]
    return gathered[...].T


def pair_rows(ref, pair):
    count = ref.shape[0] // 2
    return ref[pl.ds(pl.multiple_of(pair * count, 128), count), :]


def early_kernel(hidden_ref, beside_ref, u0, u1, out_ref, gathered):
    head = lax.axis_index("heads")
    quarter = gathered.shape[1]
    columns = pl.ds(pl.multiple_of((head ^ 2) * quarter, quarter), quarter)
    tokens = pair_tokens(hidden_ref, beside_ref, columns, gathered)
    for i, up_ref in enumerate((u0, u1)):
        out_ref[i] = jnp.dot(
            tokens, pair_rows(up_ref, head // 2), preferred_element_type=jnp.float32
        )


def give_kernel(early_ref, across_ref, diagonal_ref, u0, d0, u1, d1, out_ref, gathered):
    pair = 1 - lax.axis_index("heads") // 2
    tokens = pair_tokens(across_ref, diagonal_ref, slice(None), gathered)
    total = None
    for i, (up_ref, down_ref) in enumerate(((u0, d0), (u1, d1))):
        upward = early_ref[i] + jnp.dot(
            tokens, pair_rows(up_ref, pair), preferred_element_type=jnp.float32
        )
        part = jnp.dot(gelu(upward), down_ref[...], preferred_element_type=jnp.float32)
        part = part.astype(jnp.bfloat16).astype(jnp.float32)
        total = part if total is None else total + part
    out_ref[...] = total.astype(jnp.bfloat16)


def own_column(values_ref, rows, repeat, first):
    shape = (rows * repeat, values_ref.shape[1])
    wanted = first + lax.broadcasted_iota(jnp.int32, shape, 0) // repeat
    lane = lax.broadcasted_iota(jnp.int32, shape, 1)
    values = values_ref[...].astype(jnp.float32)
    return jnp.sum(jnp.where(lane == wanted, values, 0.0), axis=1, keepdims=True)


def keep_kernel(
    hidden_ref, beside_ref, across_ref, u0, d0, u1, d1, position_ref, length_ref, leaf_ref, parent_ref,
    out_ref, weight_ref, digits_ref, gathered,
):
    head = lax.axis_index("heads")
    rows, lanes = digits_ref.shape
    seq = out_ref.shape[0] // rows
    length = own_column(length_ref, rows, seq, head * rows)
    weight_ref[...] = jnp.where(position_ref[...] < length, 1.0 / length, 0.0)
    lane = lax.broadcasted_iota(jnp.int32, (rows, lanes), 1)
    digits = jnp.zeros((rows, lanes), jnp.int32)
    for at, (ref, first) in enumerate(
        ((leaf_ref, head * rows), (parent_ref, 0), (leaf_ref, (head ^ 1) * rows))
    ):
        values = own_column(ref, rows, 1, first).astype(jnp.int32)
        digits = jnp.where(lane == 2 * at, values % BASE, digits)
        digits = jnp.where(lane == 2 * at + 1, values // BASE, digits)
    digits_ref[...] = digits.astype(jnp.float32)
    weights = ((u0, d0), (u1, d1))
    share = hidden_ref.shape[0]
    across = (across_ref[:share, :], across_ref[share:, :])
    tokens, total = feed_forward(hidden_ref, beside_ref, across, weights, gathered, head)
    out_ref[...] = tokens.astype(jnp.float32) + total


def embed_kernel(kept_ref, came_ref, weight_ref, digits_ref, gain_ref, out_ref):
    rows, width = digits_ref.shape[0], kept_ref.shape[1]
    mixed = (kept_ref[...] + came_ref[...].astype(jnp.float32)).astype(jnp.bfloat16)
    as_float = mixed.astype(jnp.float32)
    centred = as_float - jnp.mean(as_float, axis=1, keepdims=True)
    variance = jnp.mean(centred * centred, axis=1, keepdims=True)
    weighted = centred * (lax.rsqrt(variance + 1e-05) * weight_ref[:, :1])
    pooled = jnp.sum(weighted.reshape(rows, -1, width), axis=1) * gain_ref[...]
    scale = lax.rsqrt(jnp.mean(pooled * pooled, axis=1, keepdims=True) + 1e-05)
    both = jnp.concatenate([pooled * scale, digits_ref[...]], axis=1)
    out_ref[...] = both.astype(jnp.bfloat16)


def pick_share(values, head, heads):
    share = values.shape[1] // heads
    result = values[:, :share]
    for other in range(1, heads):
        result = jnp.where(head == other, values[:, other * share : (other + 1) * share], result)
    return result


def stride_of(count):
    return STRIDE if count % STRIDE else 1


def position_of(owners, owner, lower):
    half = owners // 2
    place = 2 * ((1 - owner % 2) * half + half - 1 - owner // 2) + lower
    return place * pow(stride_of(2 * owners), -1, 2 * owners) % (2 * owners)


def owner_at(owners, block):
    half = owners // 2
    place = block * stride_of(2 * owners) % owners
    odd = jnp.where(place < half, 1, 0)
    return 2 * (half - 1 - place + (1 - odd) * half) + odd


def near_kernel(heads, leaf_count, near_ref, sum_ref, share_ref, picker_ref, parent_ref):
    leaves, width = sum_ref.shape
    count = near_ref.shape[0]
    owners = leaves // leaf_count
    digits = near_ref[:, width:].astype(jnp.float32)
    turned = digits.T
    row = lax.broadcasted_iota(jnp.int32, (leaves, count), 0)
    wanted = owner_at(owners, row // leaf_count) * leaf_count + row % leaf_count

    def pick(at):
        leaf = (turned[at : at + 1] + BASE * turned[at + 1 : at + 2]).astype(jnp.int32)
        return jnp.where(wanted == leaf, 1.0, 0.0).astype(jnp.bfloat16)

    near_sum = jnp.dot(pick(0), near_ref[:, :width], preferred_element_type=jnp.float32)
    sum_ref[...] = near_sum
    share_ref[...] = pick_share(near_sum, lax.axis_index("heads"), heads)
    picker_ref[...] = pick(4)
    digits = digits.reshape(owners, count // owners, LANES)[:, :leaf_count].reshape(leaves, LANES)
    parent = digits[:, 2:3] + BASE * digits[:, 3:4]
    parent_ref[...] = jnp.broadcast_to(parent, parent_ref.shape)


def leaf_kernel(
    heads, near_ref, far_ref, sum_ref, share_ref, picker_ref, parent_ref,
    embed_out, centers_out, parents_out, embed_ref, centers_ref, parents_ref, scratch, sems,
):
    head, index = lax.axis_index("heads"), lax.axis_index("labels")
    core = head % 2
    width = embed_ref.shape[1]
    rows = embed_ref.shape[0] // heads
    leaf_count = centers_ref.shape[0]
    owners = sum_ref.shape[0] // leaf_count
    upper, lower = position_of(owners, index, 0), position_of(owners, index, 1)

    def own_rows(ref, position, half):
        pair = pl.ds(pl.multiple_of(position // 2 * 2 * rows, 2 * rows), 2 * rows)
        return ref[pair, :width].astype(jnp.float32)[half * rows : (half + 1) * rows]

    blocks = []
    for position, half in ((lower, 1), (upper, 0)):
        near, far = own_rows(near_ref, position, half), own_rows(far_ref, position, half)
        blocks += [jnp.where(core == 0, near, far), jnp.where(core == 0, far, near)]
    embed_ref[...] = jnp.concatenate(blocks, axis=0).astype(jnp.bfloat16)
    embed_copy = pltpu.make_async_copy(embed_ref, embed_out, sems.at[0])
    embed_copy.start()
    picker = picker_ref[...]
    leaf_sum = sum_ref[...] + jnp.dot(
        picker, far_ref[:, :width], preferred_element_type=jnp.float32
    )
    far_share = pick_share(far_ref[:, :width], head, heads)
    leaf_share = share_ref[...] + jnp.dot(picker, far_share, preferred_element_type=jnp.float32)
    squares = jnp.mean(leaf_sum * leaf_sum, axis=1, keepdims=True)
    centers = leaf_share * lax.rsqrt(squares + 1e-05)
    scratch[...] = centers
    own = pl.ds(pl.multiple_of(upper // 2 * leaf_count, leaf_count), leaf_count)
    centers_ref[...] = scratch[own, :]
    centers_copy = pltpu.make_async_copy(centers_ref, centers_out, sems.at[1])
    centers_copy.start()
    parent = parent_ref[:, :1].astype(jnp.int32)
    sums = [
        jnp.sum(jnp.where(parent == index * PAR_DEV + p, centers, 0.0), axis=0, keepdims=True)
        for p in range(PAR_DEV)
    ]
    parents_ref[...] = jnp.concatenate(sums, axis=0)
    parents_copy = pltpu.make_async_copy(parents_ref, parents_out, sems.at[2])
    parents_copy.start()
    embed_copy.wait()
    centers_copy.wait()
    parents_copy.wait()


def local(owners, heads, hidden_in, w_up, w_down, norm_gain, title_length, label_leaf, leaf_parent):
    token_rows, share = hidden_in.shape
    width = w_down.shape[1]
    units = w_up.shape[1]
    labels_here = label_leaf.shape[0]
    leaf_count = leaf_parent.shape[0]
    rows = labels_here // heads
    quarter = token_rows // heads

    def swap(values, flip):
        return lax.ppermute(values, "heads", [(i, i ^ flip) for i in range(heads)])

    def array(*shape, dtype=jnp.float32):
        return jax.ShapeDtypeStruct(shape, dtype)

    hidden = hidden_in.T
    beside = swap(hidden, 1)
    position = call(
        functools.partial(position_kernel, token_rows // labels_here),
        array(quarter, LANES),
        (),
        flops=5000000000,
    )
    up_far, down_far = swap(w_up, 1), swap(w_down, 1)
    piece = array(share, quarter, dtype=jnp.bfloat16)
    across = swap(call(own_kernel, piece, (hidden, position), flops=5000000000), 2)
    near, far = call(
        merge_kernel,
        (piece, array(2 * share, quarter, dtype=jnp.bfloat16)),
        (hidden, beside),
        flops=10000000000,
    )
    diagonal = swap(near, 2)
    come_keep = swap(far, 2)
    weights = (w_up, w_down, up_far, down_far)
    cost = dict(
        scratch=[pltpu.VMEM((width, quarter), jnp.bfloat16)],
        flops=8 * quarter * width * units,
        moved=8 * width * units,
    )
    half = [pltpu.VMEM((width // 2, quarter), jnp.bfloat16)]
    early = call(
        early_kernel,
        array(2, quarter, units),
        (hidden, beside, w_up, up_far),
        scratch=half,
        flops=0,
    )
    given = call(
        give_kernel,
        array(quarter, width, dtype=jnp.bfloat16),
        (early, across, diagonal, *weights),
        scratch=half,
        flops=8 * quarter * width * units,
        moved=8 * width * units,
    )
    came = swap(given, 2)
    kept, weight, digits = call(
        keep_kernel,
        (array(quarter, width), array(quarter, LANES), array(rows, LANES)),
        (
            *(hidden, beside, come_keep, *weights, position),
            *(title_length[None, :], label_leaf[None, :], leaf_parent[None, :]),
        ),
        **dict(cost, flops=10_000_000_000),
    )
    message = call(
        embed_kernel,
        array(rows, width + LANES, dtype=jnp.bfloat16),
        (kept, came, weight, digits, norm_gain[None, :]),
    )
    groups = [
        sorted(
            range(core, owners * heads, 2),
            key=lambda rank: position_of(owners, rank // heads, 1 - rank % heads // 2),
        )
        for core in range(2)
    ]
    members = owners * heads // 2
    near = lax.all_to_all(
        jnp.broadcast_to(message[None], (members,) + message.shape),
        ("labels", "heads"),
        split_axis=0,
        concat_axis=0,
        tiled=True,
        axis_index_groups=groups,
    ).reshape(members * rows, width + LANES)
    far = swap(near, 1)
    leaves = owners * leaf_count
    ready = call(
        functools.partial(near_kernel, heads, leaf_count),
        (
            array(leaves, width),
            array(leaves, share),
            array(leaves, members * rows, dtype=jnp.bfloat16),
            array(leaves, LANES),
        ),
        (near,),
    )
    outputs = (
        array(labels_here, width, dtype=jnp.bfloat16),
        array(leaf_count, share),
        array(PAR_DEV, share),
    )
    return call(
        functools.partial(leaf_kernel, heads),
        outputs,
        (near, far, *ready),
        out_spec=HBM,
        scratch=[pltpu.VMEM(out.shape, out.dtype) for out in outputs]
        + [pltpu.VMEM((leaves, share), jnp.float32), pltpu.SemaphoreType.DMA((3,))],
    )


def solution(mesh):
    in_specs = (
        P("labels", "heads"),
        P(None, "heads"),
        P("heads", None),
        P(),
        P("labels"),
        P("labels"),
        P("labels"),
    )
    out_specs = (P("labels", None), P("labels", "heads"), P("labels", "heads"))
    body = functools.partial(local, mesh.shape["labels"], mesh.shape["heads"])
    return jax.shard_map(body, mesh=mesh, in_specs=in_specs, out_specs=out_specs, check_vma=False)
```

```python
import functools

import jax
import jax.numpy as jnp
from jax import lax
from jax.experimental import pallas as pl
from jax.experimental.pallas import tpu as pltpu
from jax.sharding import PartitionSpec as P

PAR_DEV = 2
STRIDE = 5
BASE = 128
LANES = 128
UNIT_TILE = 768
VMEM = pl.BlockSpec(memory_space=pltpu.VMEM)
HBM = pl.BlockSpec(memory_space=pl.ANY)
VMEM_LIMIT = 40 * 1024 * 1024


def call(kernel, out_shape, operands, out_spec=VMEM, scratch=(), flops=0, moved=0):
    return pl.pallas_call(
        kernel,
        out_shape=out_shape,
        in_specs=[VMEM] * len(operands),
        out_specs=jax.tree.map(lambda _: out_spec, out_shape),
        scratch_shapes=list(scratch),
        compiler_params=pltpu.CompilerParams(vmem_limit_bytes=VMEM_LIMIT),
        cost_estimate=pl.CostEstimate(flops=flops, bytes_accessed=moved, transcendentals=0),
    )(*operands)


def position_kernel(seq, out_ref):
    shape = (out_ref.shape[0], out_ref.shape[1])
    out_ref[...] = (lax.broadcasted_iota(jnp.int32, shape, 0) % seq).astype(jnp.float32)


def quarter_of(ref, owner, quarter):
    return ref[:, pl.ds(pl.multiple_of(owner * quarter, quarter), quarter)]


def own_kernel(hidden_ref, position_ref, near_ref):
    near_ref[...] = quarter_of(hidden_ref, lax.axis_index("heads"), near_ref.shape[1])


def merge_kernel(hidden_ref, beside_ref, near_ref, far_ref):
    head = lax.axis_index("heads")
    share, quarter = near_ref.shape
    near_ref[...] = quarter_of(beside_ref, head, quarter)
    far_ref[:share, :] = quarter_of(hidden_ref, head ^ 2, quarter)
    far_ref[share:, :] = quarter_of(beside_ref, head ^ 2, quarter)


def gelu(upward):
    return (0.5 * upward * (1.0 + lax.erf(upward * 0.7071067811865476))).astype(jnp.bfloat16)


def feed_forward(hidden_ref, beside_ref, across, weights, gathered, owner):
    head = lax.axis_index("heads")
    share, quarter = hidden_ref.shape[0], gathered.shape[1]
    pieces = (
        quarter_of(hidden_ref, owner, quarter),
        quarter_of(beside_ref, owner, quarter),
        *across,
    )
    for flip, piece in enumerate(pieces):
        rows = pl.ds(pl.multiple_of((head ^ flip) * share, 64), share)
        gathered[rows, :] = piece
    tokens = gathered[...].T
    total = None
    for up_ref, down_ref in weights:
        units = up_ref.shape[1]
        tile = min(UNIT_TILE, units)
        part = None
        for start in range(0, units, tile):
            upward = jnp.dot(
                tokens, up_ref[:, start : start + tile], preferred_element_type=jnp.float32
            )
            term = jnp.dot(
                gelu(upward),
                down_ref[start : start + tile, :],
                preferred_element_type=jnp.float32,
            )
            part = term if part is None else part + term
        part = part.astype(jnp.bfloat16).astype(jnp.float32)
        total = part if total is None else total + part
    return tokens, total


def pair_rows(ref, pair):
    count = ref.shape[0] // 2
    return ref[pl.ds(pl.multiple_of(pair * count, 128), count), :]


def head_rows(ref, head, share):
    return ref[pl.ds(pl.multiple_of(head * share, 64), share), :]


def early_kernel(hidden_ref, beside_ref, u0, u1, out_ref, gathered):
    head = lax.axis_index("heads")
    share, quarter = hidden_ref.shape[0], gathered.shape[1]
    for source, ref in ((head, hidden_ref), (head ^ 1, beside_ref)):
        rows = pl.ds(pl.multiple_of(source % 2 * share, 64), share)
        gathered[rows, :] = quarter_of(ref, head ^ 2, quarter)
    tokens = gathered[...].T
    for i, up_ref in enumerate((u0, u1)):
        out_ref[i] = jnp.dot(
            tokens, pair_rows(up_ref, head // 2), preferred_element_type=jnp.float32
        )


def across_kernel(early_ref, across_ref, u0, u1, out_ref):
    head = lax.axis_index("heads")
    tokens = across_ref[...].T
    for i, up_ref in enumerate((u0, u1)):
        rows = head_rows(up_ref, head ^ 2, tokens.shape[1])
        out_ref[i] = early_ref[i] + jnp.dot(tokens, rows, preferred_element_type=jnp.float32)


def give_kernel(early_ref, diagonal_ref, u0, d0, u1, d1, out_ref):
    head = lax.axis_index("heads")
    tokens = diagonal_ref[...].T
    total = None
    for i, (up_ref, down_ref) in enumerate(((u0, d0), (u1, d1))):
        rows = head_rows(up_ref, head ^ 3, tokens.shape[1])
        upward = early_ref[i] + jnp.dot(tokens, rows, preferred_element_type=jnp.float32)
        part = jnp.dot(gelu(upward), down_ref[...], preferred_element_type=jnp.float32)
        part = part.astype(jnp.bfloat16).astype(jnp.float32)
        total = part if total is None else total + part
    out_ref[...] = total.astype(jnp.bfloat16)


def own_column(values_ref, rows, repeat, first):
    shape = (rows * repeat, values_ref.shape[1])
    wanted = first + lax.broadcasted_iota(jnp.int32, shape, 0) // repeat
    lane = lax.broadcasted_iota(jnp.int32, shape, 1)
    values = values_ref[...].astype(jnp.float32)
    return jnp.sum(jnp.where(lane == wanted, values, 0.0), axis=1, keepdims=True)


def keep_kernel(
    hidden_ref, beside_ref, across_ref, u0, d0, u1, d1, position_ref, length_ref, leaf_ref, parent_ref,
    out_ref, weight_ref, digits_ref, gathered,
):
    head = lax.axis_index("heads")
    rows, lanes = digits_ref.shape
    seq = out_ref.shape[0] // rows
    length = own_column(length_ref, rows, seq, head * rows)
    weight_ref[...] = jnp.where(position_ref[...] < length, 1.0 / length, 0.0)
    lane = lax.broadcasted_iota(jnp.int32, (rows, lanes), 1)
    digits = jnp.zeros((rows, lanes), jnp.int32)
    for at, (ref, first) in enumerate(
        ((leaf_ref, head * rows), (parent_ref, 0), (leaf_ref, (head ^ 1) * rows))
    ):
        values = own_column(ref, rows, 1, first).astype(jnp.int32)
        digits = jnp.where(lane == 2 * at, values % BASE, digits)
        digits = jnp.where(lane == 2 * at + 1, values // BASE, digits)
    digits_ref[...] = digits.astype(jnp.float32)
    weights = ((u0, d0), (u1, d1))
    share = hidden_ref.shape[0]
    across = (across_ref[:share, :], across_ref[share:, :])
    tokens, total = feed_forward(hidden_ref, beside_ref, across, weights, gathered, head)
    out_ref[...] = tokens.astype(jnp.float32) + total


def embed_kernel(kept_ref, came_ref, weight_ref, digits_ref, gain_ref, out_ref):
    rows, width = digits_ref.shape[0], kept_ref.shape[1]
    mixed = (kept_ref[...] + came_ref[...].astype(jnp.float32)).astype(jnp.bfloat16)
    as_float = mixed.astype(jnp.float32)
    centred = as_float - jnp.mean(as_float, axis=1, keepdims=True)
    variance = jnp.mean(centred * centred, axis=1, keepdims=True)
    weight = jnp.concatenate([weight_ref[...]] * (width // LANES), axis=1)
    weighted = centred * weight * lax.rsqrt(variance + 1e-05)
    pooled = jnp.sum(weighted.reshape(rows, -1, width), axis=1) * gain_ref[...]
    scale = lax.rsqrt(jnp.mean(pooled * pooled, axis=1, keepdims=True) + 1e-05)
    both = jnp.concatenate([pooled * scale, digits_ref[...]], axis=1)
    out_ref[...] = both.astype(jnp.bfloat16)


def pick_share(values, head, heads):
    share = values.shape[1] // heads
    result = values[:, :share]
    for other in range(1, heads):
        result = jnp.where(head == other, values[:, other * share : (other + 1) * share], result)
    return result


def stride_of(count):
    return STRIDE if count % STRIDE else 1


def position_of(owners, owner, lower):
    half = owners // 2
    place = 2 * ((1 - owner % 2) * half + half - 1 - owner // 2) + lower
    return place * pow(stride_of(2 * owners), -1, 2 * owners) % (2 * owners)


def owner_at(owners, block):
    half = owners // 2
    place = block * stride_of(2 * owners) % owners
    odd = jnp.where(place < half, 1, 0)
    return 2 * (half - 1 - place + (1 - odd) * half) + odd


def near_kernel(heads, leaf_count, near_ref, sum_ref, share_ref, picker_ref, parent_ref):
    leaves, width = sum_ref.shape
    count = near_ref.shape[0]
    owners = leaves // leaf_count
    digits = near_ref[:, width:].astype(jnp.float32)
    turned = digits.T
    row = lax.broadcasted_iota(jnp.int32, (leaves, count), 0)
    wanted = owner_at(owners, row // leaf_count) * leaf_count + row % leaf_count

    def pick(at):
        leaf = (turned[at : at + 1] + BASE * turned[at + 1 : at + 2]).astype(jnp.int32)
        return jnp.where(wanted == leaf, 1.0, 0.0).astype(jnp.bfloat16)

    near_sum = jnp.dot(pick(0), near_ref[:, :width], preferred_element_type=jnp.float32)
    sum_ref[...] = near_sum
    share_ref[...] = pick_share(near_sum, lax.axis_index("heads"), heads)
    picker_ref[...] = pick(4)
    digits = digits.reshape(owners, count // owners, LANES)[:, :leaf_count].reshape(leaves, LANES)
    parent = digits[:, 2:3] + BASE * digits[:, 3:4]
    parent_ref[...] = jnp.broadcast_to(parent, parent_ref.shape)


def leaf_kernel(
    heads, near_ref, far_ref, sum_ref, share_ref, picker_ref, parent_ref,
    embed_out, centers_out, parents_out, embed_ref, centers_ref, parents_ref, scratch, sems,
):
    head, index = lax.axis_index("heads"), lax.axis_index("labels")
    core = head % 2
    width = embed_ref.shape[1]
    rows = embed_ref.shape[0] // heads
    leaf_count = centers_ref.shape[0]
    owners = sum_ref.shape[0] // leaf_count
    upper, lower = position_of(owners, index, 0), position_of(owners, index, 1)

    def own_rows(ref, position, half):
        pair = pl.ds(pl.multiple_of(position // 2 * 2 * rows, 2 * rows), 2 * rows)
        return ref[pair, :width].astype(jnp.float32)[half * rows : (half + 1) * rows]

    blocks = []
    for position, half in ((lower, 1), (upper, 0)):
        near, far = own_rows(near_ref, position, half), own_rows(far_ref, position, half)
        blocks += [jnp.where(core == 0, near, far), jnp.where(core == 0, far, near)]
    embed_ref[...] = jnp.concatenate(blocks, axis=0).astype(jnp.bfloat16)
    embed_copy = pltpu.make_async_copy(embed_ref, embed_out, sems.at[0])
    embed_copy.start()
    picker = picker_ref[...]
    leaf_sum = sum_ref[...] + jnp.dot(
        picker, far_ref[:, :width], preferred_element_type=jnp.float32
    )
    far_share = pick_share(far_ref[:, :width], head, heads)
    leaf_share = share_ref[...] + jnp.dot(picker, far_share, preferred_element_type=jnp.float32)
    squares = jnp.mean(leaf_sum * leaf_sum, axis=1, keepdims=True)
    centers = leaf_share * lax.rsqrt(squares + 1e-05)
    scratch[...] = centers
    own = pl.ds(pl.multiple_of(upper // 2 * leaf_count, leaf_count), leaf_count)
    centers_ref[...] = scratch[own, :]
    centers_copy = pltpu.make_async_copy(centers_ref, centers_out, sems.at[1])
    centers_copy.start()
    parent = parent_ref[:, :1].astype(jnp.int32)
    sums = [
        jnp.sum(jnp.where(parent == index * PAR_DEV + p, centers, 0.0), axis=0, keepdims=True)
        for p in range(PAR_DEV)
    ]
    parents_ref[...] = jnp.concatenate(sums, axis=0)
    parents_copy = pltpu.make_async_copy(parents_ref, parents_out, sems.at[2])
    parents_copy.start()
    embed_copy.wait()
    centers_copy.wait()
    parents_copy.wait()


def local(owners, heads, hidden_in, w_up, w_down, norm_gain, title_length, label_leaf, leaf_parent):
    token_rows, share = hidden_in.shape
    width = w_down.shape[1]
    units = w_up.shape[1]
    labels_here = label_leaf.shape[0]
    leaf_count = leaf_parent.shape[0]
    rows = labels_here // heads
    quarter = token_rows // heads

    def swap(values, flip):
        return lax.ppermute(values, "heads", [(i, i ^ flip) for i in range(heads)])

    def array(*shape, dtype=jnp.float32):
        return jax.ShapeDtypeStruct(shape, dtype)

    hidden = hidden_in.T
    beside = swap(hidden, 1)
    position = call(
        functools.partial(position_kernel, token_rows // labels_here),
        array(quarter, LANES),
        (),
        flops=5000000000,
    )
    up_far, down_far = swap(w_up, 1), swap(w_down, 1)
    piece = array(share, quarter, dtype=jnp.bfloat16)
    across = swap(call(own_kernel, piece, (hidden, position), flops=5000000000), 2)
    near, far = call(
        merge_kernel,
        (piece, array(2 * share, quarter, dtype=jnp.bfloat16)),
        (hidden, beside),
        flops=10000000000,
    )
    diagonal = swap(near, 2)
    come_keep = swap(far, 2)
    weights = (w_up, w_down, up_far, down_far)
    cost = dict(
        scratch=[pltpu.VMEM((width, quarter), jnp.bfloat16)],
        flops=8 * quarter * width * units,
        moved=8 * width * units,
    )
    upward = array(2, quarter, units)
    early = call(
        early_kernel,
        upward,
        (hidden, beside, w_up, up_far),
        scratch=[pltpu.VMEM((width // 2, quarter), jnp.bfloat16)],
    )
    early = call(across_kernel, upward, (early, across, w_up, up_far), flops=0)
    given = call(
        give_kernel,
        array(quarter, width, dtype=jnp.bfloat16),
        (early, diagonal, *weights),
        flops=8 * quarter * width * units,
        moved=8 * width * units,
    )
    came = swap(given, 2)
    kept, weight, digits = call(
        keep_kernel,
        (array(quarter, width), array(quarter, LANES), array(rows, LANES)),
        (
            *(hidden, beside, come_keep, *weights, position),
            *(title_length[None, :], label_leaf[None, :], leaf_parent[None, :]),
        ),
        **dict(cost, flops=10_000_000_000),
    )
    message = call(
        embed_kernel,
        array(rows, width + LANES, dtype=jnp.bfloat16),
        (kept, came, weight, digits, norm_gain[None, :]),
    )
    groups = [
        sorted(
            range(core, owners * heads, 2),
            key=lambda rank: position_of(owners, rank // heads, 1 - rank % heads // 2),
        )
        for core in range(2)
    ]
    members = owners * heads // 2
    near = lax.all_to_all(
        jnp.broadcast_to(message[None], (members,) + message.shape),
        ("labels", "heads"),
        split_axis=0,
        concat_axis=0,
        tiled=True,
        axis_index_groups=groups,
    ).reshape(members * rows, width + LANES)
    far = swap(near, 1)
    leaves = owners * leaf_count
    ready = call(
        functools.partial(near_kernel, heads, leaf_count),
        (
            array(leaves, width),
            array(leaves, share),
            array(leaves, members * rows, dtype=jnp.bfloat16),
            array(leaves, LANES),
        ),
        (near,),
    )
    outputs = (
        array(labels_here, width, dtype=jnp.bfloat16),
        array(leaf_count, share),
        array(PAR_DEV, share),
    )
    return call(
        functools.partial(leaf_kernel, heads),
        outputs,
        (near, far, *ready),
        out_spec=HBM,
        scratch=[pltpu.VMEM(out.shape, out.dtype) for out in outputs]
        + [pltpu.VMEM((leaves, share), jnp.float32), pltpu.SemaphoreType.DMA((3,))],
    )


def solution(mesh):
    in_specs = (
        P("labels", "heads"),
        P(None, "heads"),
        P("heads", None),
        P(),
        P("labels"),
        P("labels"),
        P("labels"),
    )
    out_specs = (P("labels", None), P("labels", "heads"), P("labels", "heads"))
    body = functools.partial(local, mesh.shape["labels"], mesh.shape["heads"])
    return jax.shard_map(body, mesh=mesh, in_specs=in_specs, out_specs=out_specs, check_vma=False)
```

```python
import functools

import jax
import jax.numpy as jnp
from jax import lax
from jax.experimental import pallas as pl
from jax.experimental.pallas import tpu as pltpu
from jax.sharding import PartitionSpec as P

PAR_DEV = 2
STRIDE = 5
BASE = 128
LANES = 128
UNIT_TILE = 768
VMEM = pl.BlockSpec(memory_space=pltpu.VMEM)
HBM = pl.BlockSpec(memory_space=pl.ANY)
VMEM_LIMIT = 40 * 1024 * 1024


def call(kernel, out_shape, operands, out_spec=VMEM, scratch=(), flops=0, moved=0):
    return pl.pallas_call(
        kernel,
        out_shape=out_shape,
        in_specs=[VMEM] * len(operands),
        out_specs=jax.tree.map(lambda _: out_spec, out_shape),
        scratch_shapes=list(scratch),
        compiler_params=pltpu.CompilerParams(vmem_limit_bytes=VMEM_LIMIT),
        cost_estimate=pl.CostEstimate(flops=flops, bytes_accessed=moved, transcendentals=0),
    )(*operands)


def position_kernel(seq, out_ref):
    shape = (out_ref.shape[0], out_ref.shape[1])
    out_ref[...] = (lax.broadcasted_iota(jnp.int32, shape, 0) % seq).astype(jnp.float32)


def quarter_of(ref, owner, quarter):
    return ref[:, pl.ds(pl.multiple_of(owner * quarter, quarter), quarter)]


def own_kernel(hidden_ref, position_ref, near_ref):
    near_ref[...] = quarter_of(hidden_ref, lax.axis_index("heads"), near_ref.shape[1])


def merge_kernel(hidden_ref, beside_ref, near_ref, far_ref):
    head = lax.axis_index("heads")
    share, quarter = near_ref.shape
    near_ref[...] = quarter_of(beside_ref, head, quarter)
    far_ref[:share, :] = quarter_of(hidden_ref, head ^ 2, quarter)
    far_ref[share:, :] = quarter_of(beside_ref, head ^ 2, quarter)


def gelu(upward):
    return (0.5 * upward * (1.0 + lax.erf(upward * 0.7071067811865476))).astype(jnp.bfloat16)


def feed_forward(hidden_ref, beside_ref, across, weights, gathered, owner):
    head = lax.axis_index("heads")
    share, quarter = hidden_ref.shape[0], gathered.shape[1]
    pieces = (
        quarter_of(hidden_ref, owner, quarter),
        quarter_of(beside_ref, owner, quarter),
        *across,
    )
    for flip, piece in enumerate(pieces):
        rows = pl.ds(pl.multiple_of((head ^ flip) * share, 64), share)
        gathered[rows, :] = piece
    tokens = gathered[...].T
    total = None
    for up_ref, down_ref in weights:
        units = up_ref.shape[1]
        tile = min(UNIT_TILE, units)
        part = None
        for start in range(0, units, tile):
            upward = jnp.dot(
                tokens, up_ref[:, start : start + tile], preferred_element_type=jnp.float32
            )
            term = jnp.dot(
                gelu(upward),
                down_ref[start : start + tile, :],
                preferred_element_type=jnp.float32,
            )
            part = term if part is None else part + term
        part = part.astype(jnp.bfloat16).astype(jnp.float32)
        total = part if total is None else total + part
    return tokens, total


def pair_rows(ref, pair):
    count = ref.shape[0] // 2
    return ref[pl.ds(pl.multiple_of(pair * count, 128), count), :]


def head_rows(ref, head, share):
    return ref[pl.ds(pl.multiple_of(head * share, 64), share), :]


def early_kernel(hidden_ref, beside_ref, u0, u1, out_ref, gathered):
    head = lax.axis_index("heads")
    share, quarter = hidden_ref.shape[0], gathered.shape[1]
    for source, ref in ((head, hidden_ref), (head ^ 1, beside_ref)):
        rows = pl.ds(pl.multiple_of(source % 2 * share, 64), share)
        gathered[rows, :] = quarter_of(ref, head ^ 2, quarter)
    tokens = gathered[...].T
    for i, up_ref in enumerate((u0, u1)):
        out_ref[i] = jnp.dot(
            tokens, pair_rows(up_ref, head // 2), preferred_element_type=jnp.float32
        )


def across_kernel(early_ref, across_ref, u0, u1, out_ref):
    head = lax.axis_index("heads")
    tokens = across_ref[...].T
    for i, up_ref in enumerate((u0, u1)):
        rows = head_rows(up_ref, head ^ 2, tokens.shape[1])
        out_ref[i] = early_ref[i] + jnp.dot(tokens, rows, preferred_element_type=jnp.float32)


def give_kernel(early_ref, diagonal_ref, u0, d0, u1, d1, out_ref):
    head = lax.axis_index("heads")
    tokens = diagonal_ref[...].T
    total = None
    for i, (up_ref, down_ref) in enumerate(((u0, d0), (u1, d1))):
        rows = head_rows(up_ref, head ^ 3, tokens.shape[1])
        upward = early_ref[i] + jnp.dot(tokens, rows, preferred_element_type=jnp.float32)
        part = jnp.dot(gelu(upward), down_ref[...], preferred_element_type=jnp.float32)
        part = part.astype(jnp.bfloat16).astype(jnp.float32)
        total = part if total is None else total + part
    out_ref[...] = total.astype(jnp.bfloat16)


def own_column(values_ref, rows, repeat, first):
    shape = (rows * repeat, values_ref.shape[1])
    wanted = first + lax.broadcasted_iota(jnp.int32, shape, 0) // repeat
    lane = lax.broadcasted_iota(jnp.int32, shape, 1)
    values = values_ref[...].astype(jnp.float32)
    return jnp.sum(jnp.where(lane == wanted, values, 0.0), axis=1, keepdims=True)


def keep_kernel(
    hidden_ref, beside_ref, across_ref, u0, d0, u1, d1, position_ref, length_ref, leaf_ref, parent_ref,
    out_ref, weight_ref, digits_ref, gathered,
):
    head = lax.axis_index("heads")
    rows, lanes = digits_ref.shape
    seq = out_ref.shape[0] // rows
    length = own_column(length_ref, rows, seq, head * rows)
    weight_ref[...] = jnp.where(position_ref[...] < length, 1.0 / length, 0.0)
    lane = lax.broadcasted_iota(jnp.int32, (rows, lanes), 1)
    digits = jnp.zeros((rows, lanes), jnp.int32)
    for at, (ref, first) in enumerate(
        ((leaf_ref, head * rows), (parent_ref, 0), (leaf_ref, (head ^ 1) * rows))
    ):
        values = own_column(ref, rows, 1, first).astype(jnp.int32)
        digits = jnp.where(lane == 2 * at, values % BASE, digits)
        digits = jnp.where(lane == 2 * at + 1, values // BASE, digits)
    digits_ref[...] = digits.astype(jnp.float32)
    weights = ((u0, d0), (u1, d1))
    share = hidden_ref.shape[0]
    across = (across_ref[:share, :], across_ref[share:, :])
    tokens, total = feed_forward(hidden_ref, beside_ref, across, weights, gathered, head)
    out_ref[...] = tokens.astype(jnp.float32) + total


def embed_kernel(kept_ref, came_ref, weight_ref, digits_ref, gain_ref, out_ref):
    rows, width = digits_ref.shape[0], kept_ref.shape[1]
    mixed = (kept_ref[...] + came_ref[...].astype(jnp.float32)).astype(jnp.bfloat16)
    as_float = mixed.astype(jnp.float32)
    centred = as_float - jnp.mean(as_float, axis=1, keepdims=True)
    variance = jnp.mean(centred * centred, axis=1, keepdims=True)
    weight = jnp.concatenate([weight_ref[...]] * (width // LANES), axis=1)
    weighted = centred * weight * lax.rsqrt(variance + 1e-05)
    pooled = jnp.sum(weighted.reshape(rows, -1, width), axis=1) * gain_ref[...]
    scale = lax.rsqrt(jnp.mean(pooled * pooled, axis=1, keepdims=True) + 1e-05)
    both = jnp.concatenate([pooled * scale, digits_ref[...]], axis=1)
    both = both.astype(jnp.bfloat16)
    for i in range(out_ref.shape[0]):
        out_ref[i] = both


def pick_share(values, head, heads):
    share = values.shape[1] // heads
    result = values[:, :share]
    for other in range(1, heads):
        result = jnp.where(head == other, values[:, other * share : (other + 1) * share], result)
    return result


def stride_of(count):
    return STRIDE if count % STRIDE else 1


def position_of(owners, owner, lower):
    half = owners // 2
    place = 2 * ((1 - owner % 2) * half + half - 1 - owner // 2) + lower
    return place * pow(stride_of(2 * owners), -1, 2 * owners) % (2 * owners)


def owner_at(owners, block):
    half = owners // 2
    place = block * stride_of(2 * owners) % owners
    odd = jnp.where(place < half, 1, 0)
    return 2 * (half - 1 - place + (1 - odd) * half) + odd


def near_kernel(heads, leaf_count, near_ref, sum_ref, share_ref, picker_ref, parent_ref):
    leaves, width = sum_ref.shape
    count = near_ref.shape[0]
    owners = leaves // leaf_count
    digits = near_ref[:, width:].astype(jnp.float32)
    turned = digits.T
    row = lax.broadcasted_iota(jnp.int32, (leaves, count), 0)
    wanted = owner_at(owners, row // leaf_count) * leaf_count + row % leaf_count

    def pick(at):
        leaf = (turned[at : at + 1] + BASE * turned[at + 1 : at + 2]).astype(jnp.int32)
        return jnp.where(wanted == leaf, 1.0, 0.0).astype(jnp.bfloat16)

    near_sum = jnp.dot(pick(0), near_ref[:, :width], preferred_element_type=jnp.float32)
    sum_ref[...] = near_sum
    share_ref[...] = pick_share(near_sum, lax.axis_index("heads"), heads)
    picker_ref[...] = pick(4)
    digits = digits.reshape(owners, count // owners, LANES)[:, :leaf_count].reshape(leaves, LANES)
    parent = digits[:, 2:3] + BASE * digits[:, 3:4]
    parent_ref[...] = jnp.broadcast_to(parent, parent_ref.shape)


def leaf_kernel(
    heads, near_ref, far_ref, sum_ref, share_ref, picker_ref, parent_ref,
    embed_out, centers_out, parents_out, embed_ref, centers_ref, parents_ref, scratch, sems,
):
    head, index = lax.axis_index("heads"), lax.axis_index("labels")
    core = head % 2
    width = embed_ref.shape[1]
    rows = embed_ref.shape[0] // heads
    leaf_count = centers_ref.shape[0]
    owners = sum_ref.shape[0] // leaf_count
    upper, lower = position_of(owners, index, 0), position_of(owners, index, 1)

    def own_rows(ref, position, half):
        pair = pl.ds(pl.multiple_of(position // 2 * 2 * rows, 2 * rows), 2 * rows)
        return ref[pair, :width].astype(jnp.float32)[half * rows : (half + 1) * rows]

    blocks = []
    for position, half in ((lower, 1), (upper, 0)):
        near, far = own_rows(near_ref, position, half), own_rows(far_ref, position, half)
        blocks += [jnp.where(core == 0, near, far), jnp.where(core == 0, far, near)]
    embed_ref[...] = jnp.concatenate(blocks, axis=0).astype(jnp.bfloat16)
    embed_copy = pltpu.make_async_copy(embed_ref, embed_out, sems.at[0])
    embed_copy.start()
    picker = picker_ref[...]
    leaf_sum = sum_ref[...] + jnp.dot(
        picker, far_ref[:, :width], preferred_element_type=jnp.float32
    )
    far_share = pick_share(far_ref[:, :width], head, heads)
    leaf_share = share_ref[...] + jnp.dot(picker, far_share, preferred_element_type=jnp.float32)
    squares = jnp.mean(leaf_sum * leaf_sum, axis=1, keepdims=True)
    centers = leaf_share * lax.rsqrt(squares + 1e-05)
    scratch[...] = centers
    own = pl.ds(pl.multiple_of(upper // 2 * leaf_count, leaf_count), leaf_count)
    centers_ref[...] = scratch[own, :]
    centers_copy = pltpu.make_async_copy(centers_ref, centers_out, sems.at[1])
    centers_copy.start()
    parent = parent_ref[:, :1].astype(jnp.int32)
    sums = [
        jnp.sum(jnp.where(parent == index * PAR_DEV + p, centers, 0.0), axis=0, keepdims=True)
        for p in range(PAR_DEV)
    ]
    parents_ref[...] = jnp.concatenate(sums, axis=0)
    parents_copy = pltpu.make_async_copy(parents_ref, parents_out, sems.at[2])
    parents_copy.start()
    embed_copy.wait()
    centers_copy.wait()
    parents_copy.wait()


def local(owners, heads, hidden_in, w_up, w_down, norm_gain, title_length, label_leaf, leaf_parent):
    token_rows, share = hidden_in.shape
    width = w_down.shape[1]
    units = w_up.shape[1]
    labels_here = label_leaf.shape[0]
    leaf_count = leaf_parent.shape[0]
    rows = labels_here // heads
    quarter = token_rows // heads

    def swap(values, flip):
        return lax.ppermute(values, "heads", [(i, i ^ flip) for i in range(heads)])

    def array(*shape, dtype=jnp.float32):
        return jax.ShapeDtypeStruct(shape, dtype)

    hidden = hidden_in.T
    beside = swap(hidden, 1)
    position = call(
        functools.partial(position_kernel, token_rows // labels_here),
        array(quarter, LANES),
        (),
        flops=5000000000,
    )
    up_far, down_far = swap(w_up, 1), swap(w_down, 1)
    piece = array(share, quarter, dtype=jnp.bfloat16)
    across = swap(call(own_kernel, piece, (hidden, position), flops=5000000000), 2)
    near, far = call(
        merge_kernel,
        (piece, array(2 * share, quarter, dtype=jnp.bfloat16)),
        (hidden, beside),
        flops=10000000000,
    )
    diagonal = swap(near, 2)
    come_keep = swap(far, 2)
    weights = (w_up, w_down, up_far, down_far)
    cost = dict(
        scratch=[pltpu.VMEM((width, quarter), jnp.bfloat16)],
        flops=8 * quarter * width * units,
        moved=8 * width * units,
    )
    upward = array(2, quarter, units)
    early = call(
        early_kernel,
        upward,
        (hidden, beside, w_up, up_far),
        scratch=[pltpu.VMEM((width // 2, quarter), jnp.bfloat16)],
    )
    early = call(across_kernel, upward, (early, across, w_up, up_far), flops=0)
    given = call(
        give_kernel,
        array(quarter, width, dtype=jnp.bfloat16),
        (early, diagonal, *weights),
        flops=8 * quarter * width * units,
        moved=8 * width * units,
    )
    came = swap(given, 2)
    kept, weight, digits = call(
        keep_kernel,
        (array(quarter, width), array(quarter, LANES), array(rows, LANES)),
        (
            *(hidden, beside, come_keep, *weights, position),
            *(title_length[None, :], label_leaf[None, :], leaf_parent[None, :]),
        ),
        **dict(cost, flops=10_000_000_000),
    )
    message = call(
        embed_kernel,
        array(owners * heads // 2, rows, width + LANES, dtype=jnp.bfloat16),
        (kept, came, weight, digits, norm_gain[None, :]),
    )
    groups = [
        sorted(
            range(core, owners * heads, 2),
            key=lambda rank: position_of(owners, rank // heads, 1 - rank % heads // 2),
        )
        for core in range(2)
    ]
    members = owners * heads // 2
    near = lax.all_to_all(
        message,
        ("labels", "heads"),
        split_axis=0,
        concat_axis=0,
        tiled=True,
        axis_index_groups=groups,
    ).reshape(members * rows, width + LANES)
    far = swap(near, 1)
    leaves = owners * leaf_count
    ready = call(
        functools.partial(near_kernel, heads, leaf_count),
        (
            array(leaves, width),
            array(leaves, share),
            array(leaves, members * rows, dtype=jnp.bfloat16),
            array(leaves, LANES),
        ),
        (near,),
    )
    outputs = (
        array(labels_here, width, dtype=jnp.bfloat16),
        array(leaf_count, share),
        array(PAR_DEV, share),
    )
    return call(
        functools.partial(leaf_kernel, heads),
        outputs,
        (near, far, *ready),
        out_spec=HBM,
        scratch=[pltpu.VMEM(out.shape, out.dtype) for out in outputs]
        + [pltpu.VMEM((leaves, share), jnp.float32), pltpu.SemaphoreType.DMA((3,))],
    )


def solution(mesh):
    in_specs = (
        P("labels", "heads"),
        P(None, "heads"),
        P("heads", None),
        P(),
        P("labels"),
        P("labels"),
        P("labels"),
    )
    out_specs = (P("labels", None), P("labels", "heads"), P("labels", "heads"))
    body = functools.partial(local, mesh.shape["labels"], mesh.shape["heads"])
    return jax.shard_map(body, mesh=mesh, in_specs=in_specs, out_specs=out_specs, check_vma=False)
```

```python
import functools

import jax
import jax.numpy as jnp
from jax import lax
from jax.experimental import pallas as pl
from jax.experimental.pallas import tpu as pltpu
from jax.sharding import PartitionSpec as P

PAR_DEV = 2
STRIDE = 5
BASE = 128
LANES = 128
UNIT_TILE = 768
VMEM = pl.BlockSpec(memory_space=pltpu.VMEM)
HBM = pl.BlockSpec(memory_space=pl.ANY)
VMEM_LIMIT = 40 * 1024 * 1024


def call(kernel, out_shape, operands, out_spec=VMEM, scratch=(), flops=0, moved=0):
    return pl.pallas_call(
        kernel,
        out_shape=out_shape,
        in_specs=[VMEM] * len(operands),
        out_specs=jax.tree.map(lambda _: out_spec, out_shape),
        scratch_shapes=list(scratch),
        compiler_params=pltpu.CompilerParams(vmem_limit_bytes=VMEM_LIMIT),
        cost_estimate=pl.CostEstimate(flops=flops, bytes_accessed=moved, transcendentals=0),
    )(*operands)


def position_kernel(seq, out_ref):
    shape = (out_ref.shape[0], out_ref.shape[1])
    out_ref[...] = (lax.broadcasted_iota(jnp.int32, shape, 0) % seq).astype(jnp.float32)


def quarter_of(ref, owner, quarter):
    return ref[:, pl.ds(pl.multiple_of(owner * quarter, quarter), quarter)]


def own_kernel(hidden_ref, position_ref, near_ref):
    near_ref[...] = quarter_of(hidden_ref, lax.axis_index("heads"), near_ref.shape[1])


def merge_kernel(hidden_ref, beside_ref, near_ref, far_ref):
    head = lax.axis_index("heads")
    share, quarter = near_ref.shape
    near_ref[...] = quarter_of(beside_ref, head, quarter)
    far_ref[:share, :] = quarter_of(hidden_ref, head ^ 2, quarter)
    far_ref[share:, :] = quarter_of(beside_ref, head ^ 2, quarter)


def gelu(upward):
    return (0.5 * upward * (1.0 + lax.erf(upward * 0.7071067811865476))).astype(jnp.bfloat16)


def feed_forward(hidden_ref, beside_ref, across, weights, gathered, owner):
    head = lax.axis_index("heads")
    share, quarter = hidden_ref.shape[0], gathered.shape[1]
    pieces = (
        quarter_of(hidden_ref, owner, quarter),
        quarter_of(beside_ref, owner, quarter),
        *across,
    )
    for flip, piece in enumerate(pieces):
        rows = pl.ds(pl.multiple_of((head ^ flip) * share, 64), share)
        gathered[rows, :] = piece
    tokens = gathered[...].T
    total = None
    for up_ref, down_ref in weights:
        units = up_ref.shape[1]
        tile = min(UNIT_TILE, units)
        part = None
        for start in range(0, units, tile):
            upward = jnp.dot(
                tokens, up_ref[:, start : start + tile], preferred_element_type=jnp.float32
            )
            term = jnp.dot(
                gelu(upward),
                down_ref[start : start + tile, :],
                preferred_element_type=jnp.float32,
            )
            part = term if part is None else part + term
        part = part.astype(jnp.bfloat16).astype(jnp.float32)
        total = part if total is None else total + part
    return tokens, total


def pair_rows(ref, pair):
    count = ref.shape[0] // 2
    return ref[pl.ds(pl.multiple_of(pair * count, 128), count), :]


def head_rows(ref, head, share):
    return ref[pl.ds(pl.multiple_of(head * share, 64), share), :]


def early_kernel(hidden_ref, beside_ref, u0, u1, out_ref, gathered):
    head = lax.axis_index("heads")
    share, quarter = hidden_ref.shape[0], gathered.shape[1]
    for source, ref in ((head, hidden_ref), (head ^ 1, beside_ref)):
        rows = pl.ds(pl.multiple_of(source % 2 * share, 64), share)
        gathered[rows, :] = quarter_of(ref, head ^ 2, quarter)
    tokens = gathered[...].T
    for i, up_ref in enumerate((u0, u1)):
        out_ref[i] = jnp.dot(
            tokens, pair_rows(up_ref, head // 2), preferred_element_type=jnp.float32
        )


def across_kernel(early_ref, across_ref, u0, u1, out_ref):
    head = lax.axis_index("heads")
    tokens = across_ref[...].T
    for i, up_ref in enumerate((u0, u1)):
        rows = head_rows(up_ref, head ^ 2, tokens.shape[1])
        out_ref[i] = early_ref[i] + jnp.dot(tokens, rows, preferred_element_type=jnp.float32)


def give_kernel(early_ref, diagonal_ref, u0, d0, u1, d1, out_ref):
    head = lax.axis_index("heads")
    tokens = diagonal_ref[...].T
    total = None
    for i, (up_ref, down_ref) in enumerate(((u0, d0), (u1, d1))):
        rows = head_rows(up_ref, head ^ 3, tokens.shape[1])
        upward = early_ref[i] + jnp.dot(tokens, rows, preferred_element_type=jnp.float32)
        part = jnp.dot(gelu(upward), down_ref[...], preferred_element_type=jnp.float32)
        part = part.astype(jnp.bfloat16).astype(jnp.float32)
        total = part if total is None else total + part
    out_ref[...] = total.astype(jnp.bfloat16)


def own_column(values_ref, rows, repeat, first):
    shape = (rows * repeat, values_ref.shape[1])
    wanted = first + lax.broadcasted_iota(jnp.int32, shape, 0) // repeat
    lane = lax.broadcasted_iota(jnp.int32, shape, 1)
    values = values_ref[...].astype(jnp.float32)
    return jnp.sum(jnp.where(lane == wanted, values, 0.0), axis=1, keepdims=True)


def keep_kernel(
    hidden_ref, beside_ref, across_ref, u0, d0, u1, d1, position_ref, length_ref, leaf_ref, parent_ref,
    out_ref, weight_ref, digits_ref, gathered,
):
    head = lax.axis_index("heads")
    rows, lanes = digits_ref.shape
    seq = out_ref.shape[0] // rows
    length = own_column(length_ref, rows, seq, head * rows)
    weight_ref[...] = jnp.where(position_ref[...] < length, 1.0 / length, 0.0)
    lane = lax.broadcasted_iota(jnp.int32, (rows, lanes), 1)
    digits = jnp.zeros((rows, lanes), jnp.int32)
    for at, (ref, first) in enumerate(
        ((leaf_ref, head * rows), (parent_ref, 0), (leaf_ref, (head ^ 1) * rows))
    ):
        values = own_column(ref, rows, 1, first).astype(jnp.int32)
        digits = jnp.where(lane == 2 * at, values % BASE, digits)
        digits = jnp.where(lane == 2 * at + 1, values // BASE, digits)
    digits_ref[...] = digits.astype(jnp.float32)
    weights = ((u0, d0), (u1, d1))
    share = hidden_ref.shape[0]
    across = (across_ref[:share, :], across_ref[share:, :])
    tokens, total = feed_forward(hidden_ref, beside_ref, across, weights, gathered, head)
    out_ref[...] = tokens.astype(jnp.float32) + total


def embed_kernel(kept_ref, came_ref, weight_ref, digits_ref, gain_ref, out_ref):
    rows, width = digits_ref.shape[0], kept_ref.shape[1]
    mixed = (kept_ref[...] + came_ref[...].astype(jnp.float32)).astype(jnp.bfloat16)
    as_float = mixed.astype(jnp.float32)
    centred = as_float - jnp.mean(as_float, axis=1, keepdims=True)
    variance = jnp.mean(centred * centred, axis=1, keepdims=True)
    weight = jnp.concatenate([weight_ref[...]] * (width // LANES), axis=1)
    weighted = centred * weight * lax.rsqrt(variance + 1e-05)
    pooled = jnp.sum(weighted.reshape(rows, -1, width), axis=1) * gain_ref[...]
    scale = lax.rsqrt(jnp.mean(pooled * pooled, axis=1, keepdims=True) + 1e-05)
    both = jnp.concatenate([pooled * scale, digits_ref[...]], axis=1)
    both = both.astype(jnp.bfloat16)
    for i in range(out_ref.shape[0]):
        out_ref[i] = both


def pick_share(values, head, heads):
    share = values.shape[1] // heads
    result = values[:, :share]
    for other in range(1, heads):
        result = jnp.where(head == other, values[:, other * share : (other + 1) * share], result)
    return result


def stride_of(count):
    return STRIDE if count % STRIDE else 1


def position_of(owners, owner, lower):
    half = owners // 2
    place = 2 * ((1 - owner % 2) * half + half - 1 - owner // 2) + lower
    return place * pow(stride_of(2 * owners), -1, 2 * owners) % (2 * owners)


def owner_at(owners, block):
    half = owners // 2
    place = block * stride_of(2 * owners) % owners
    odd = jnp.where(place < half, 1, 0)
    return 2 * (half - 1 - place + (1 - odd) * half) + odd


def own_rows(ref, position, half, rows, width):
    pair = pl.ds(pl.multiple_of(position // 2 * 2 * rows, 2 * rows), 2 * rows)
    return ref[pair, :width].astype(jnp.float32)[half * rows : (half + 1) * rows]


def near_kernel(
    heads, leaf_count, near_ref, sum_ref, share_ref, picker_ref, parent_ref, own_ref
):
    leaves, width = sum_ref.shape
    count = near_ref.shape[0]
    owners = leaves // leaf_count
    digits = near_ref[:, width:].astype(jnp.float32)
    turned = digits.T
    row = lax.broadcasted_iota(jnp.int32, (leaves, count), 0)
    wanted = owner_at(owners, row // leaf_count) * leaf_count + row % leaf_count

    def pick(at):
        leaf = (turned[at : at + 1] + BASE * turned[at + 1 : at + 2]).astype(jnp.int32)
        return jnp.where(wanted == leaf, 1.0, 0.0).astype(jnp.bfloat16)

    near_sum = jnp.dot(pick(0), near_ref[:, :width], preferred_element_type=jnp.float32)
    sum_ref[...] = near_sum
    share_ref[...] = pick_share(near_sum, lax.axis_index("heads"), heads)
    picker_ref[...] = pick(4)
    digits = digits.reshape(owners, count // owners, LANES)[:, :leaf_count].reshape(leaves, LANES)
    parent = digits[:, 2:3] + BASE * digits[:, 3:4]
    parent_ref[...] = jnp.broadcast_to(parent, parent_ref.shape)
    rows = own_ref.shape[0] // 2
    for i in range(2):
        position = position_of(owners, lax.axis_index("labels"), 1 - i)
        own_ref[i * rows : (i + 1) * rows, :] = own_rows(near_ref, position, 1 - i, rows, width)


def leaf_kernel(
    heads, far_ref, sum_ref, share_ref, picker_ref, parent_ref, own_ref,
    embed_out, centers_out, parents_out, embed_ref, centers_ref, parents_ref, scratch, sems,
):
    head, index = lax.axis_index("heads"), lax.axis_index("labels")
    core = head % 2
    width = embed_ref.shape[1]
    rows = embed_ref.shape[0] // heads
    leaf_count = centers_ref.shape[0]
    owners = sum_ref.shape[0] // leaf_count
    upper, lower = position_of(owners, index, 0), position_of(owners, index, 1)

    blocks = []
    for i, position in enumerate((lower, upper)):
        near = own_ref[i * rows : (i + 1) * rows, :]
        far = own_rows(far_ref, position, 1 - i, rows, width)
        blocks += [jnp.where(core == 0, near, far), jnp.where(core == 0, far, near)]
    embed_ref[...] = jnp.concatenate(blocks, axis=0).astype(jnp.bfloat16)
    embed_copy = pltpu.make_async_copy(embed_ref, embed_out, sems.at[0])
    embed_copy.start()
    picker = picker_ref[...]
    leaf_sum = sum_ref[...] + jnp.dot(
        picker, far_ref[:, :width], preferred_element_type=jnp.float32
    )
    far_share = pick_share(far_ref[:, :width], head, heads)
    leaf_share = share_ref[...] + jnp.dot(picker, far_share, preferred_element_type=jnp.float32)
    squares = jnp.mean(leaf_sum * leaf_sum, axis=1, keepdims=True)
    centers = leaf_share * lax.rsqrt(squares + 1e-05)
    scratch[...] = centers
    own = pl.ds(pl.multiple_of(upper // 2 * leaf_count, leaf_count), leaf_count)
    centers_ref[...] = scratch[own, :]
    centers_copy = pltpu.make_async_copy(centers_ref, centers_out, sems.at[1])
    centers_copy.start()
    parent = parent_ref[:, :1].astype(jnp.int32)
    sums = [
        jnp.sum(jnp.where(parent == index * PAR_DEV + p, centers, 0.0), axis=0, keepdims=True)
        for p in range(PAR_DEV)
    ]
    parents_ref[...] = jnp.concatenate(sums, axis=0)
    parents_copy = pltpu.make_async_copy(parents_ref, parents_out, sems.at[2])
    parents_copy.start()
    embed_copy.wait()
    centers_copy.wait()
    parents_copy.wait()


def local(owners, heads, hidden_in, w_up, w_down, norm_gain, title_length, label_leaf, leaf_parent):
    token_rows, share = hidden_in.shape
    width = w_down.shape[1]
    units = w_up.shape[1]
    labels_here = label_leaf.shape[0]
    leaf_count = leaf_parent.shape[0]
    rows = labels_here // heads
    quarter = token_rows // heads

    def swap(values, flip):
        return lax.ppermute(values, "heads", [(i, i ^ flip) for i in range(heads)])

    def array(*shape, dtype=jnp.float32):
        return jax.ShapeDtypeStruct(shape, dtype)

    hidden = hidden_in.T
    beside = swap(hidden, 1)
    position = call(
        functools.partial(position_kernel, token_rows // labels_here),
        array(quarter, LANES),
        (),
        flops=5000000000,
    )
    up_far, down_far = swap(w_up, 1), swap(w_down, 1)
    piece = array(share, quarter, dtype=jnp.bfloat16)
    across = swap(call(own_kernel, piece, (hidden, position), flops=5000000000), 2)
    near, far = call(
        merge_kernel,
        (piece, array(2 * share, quarter, dtype=jnp.bfloat16)),
        (hidden, beside),
        flops=10000000000,
    )
    diagonal = swap(near, 2)
    come_keep = swap(far, 2)
    weights = (w_up, w_down, up_far, down_far)
    cost = dict(
        scratch=[pltpu.VMEM((width, quarter), jnp.bfloat16)],
        flops=8 * quarter * width * units,
        moved=8 * width * units,
    )
    upward = array(2, quarter, units)
    early = call(
        early_kernel,
        upward,
        (hidden, beside, w_up, up_far),
        scratch=[pltpu.VMEM((width // 2, quarter), jnp.bfloat16)],
    )
    early = call(across_kernel, upward, (early, across, w_up, up_far), flops=0)
    given = call(
        give_kernel,
        array(quarter, width, dtype=jnp.bfloat16),
        (early, diagonal, *weights),
        flops=8 * quarter * width * units,
        moved=8 * width * units,
    )
    came = swap(given, 2)
    kept, weight, digits = call(
        keep_kernel,
        (array(quarter, width), array(quarter, LANES), array(rows, LANES)),
        (
            *(hidden, beside, come_keep, *weights, position),
            *(title_length[None, :], label_leaf[None, :], leaf_parent[None, :]),
        ),
        **dict(cost, flops=10_000_000_000),
    )
    message = call(
        embed_kernel,
        array(owners * heads // 2, rows, width + LANES, dtype=jnp.bfloat16),
        (kept, came, weight, digits, norm_gain[None, :]),
    )
    groups = [
        sorted(
            range(core, owners * heads, 2),
            key=lambda rank: position_of(owners, rank // heads, 1 - rank % heads // 2),
        )
        for core in range(2)
    ]
    members = owners * heads // 2
    near = lax.all_to_all(
        message,
        ("labels", "heads"),
        split_axis=0,
        concat_axis=0,
        tiled=True,
        axis_index_groups=groups,
    ).reshape(members * rows, width + LANES)
    far = swap(near, 1)
    leaves = owners * leaf_count
    ready = call(
        functools.partial(near_kernel, heads, leaf_count),
        (
            array(leaves, width),
            array(leaves, share),
            array(leaves, members * rows, dtype=jnp.bfloat16),
            array(leaves, LANES),
            array(2 * rows, width),
        ),
        (near,),
    )
    outputs = (
        array(labels_here, width, dtype=jnp.bfloat16),
        array(leaf_count, share),
        array(PAR_DEV, share),
    )
    return call(
        functools.partial(leaf_kernel, heads),
        outputs,
        (far, *ready),
        out_spec=HBM,
        scratch=[pltpu.VMEM(out.shape, out.dtype) for out in outputs]
        + [pltpu.VMEM((leaves, share), jnp.float32), pltpu.SemaphoreType.DMA((3,))],
    )


def solution(mesh):
    in_specs = (
        P("labels", "heads"),
        P(None, "heads"),
        P("heads", None),
        P(),
        P("labels"),
        P("labels"),
        P("labels"),
    )
    out_specs = (P("labels", None), P("labels", "heads"), P("labels", "heads"))
    body = functools.partial(local, mesh.shape["labels"], mesh.shape["heads"])
    return jax.shard_map(body, mesh=mesh, in_specs=in_specs, out_specs=out_specs, check_vma=False)
```

```python
import functools

import jax
import jax.numpy as jnp
from jax import lax
from jax.experimental import pallas as pl
from jax.experimental.pallas import tpu as pltpu
from jax.sharding import PartitionSpec as P

PAR_DEV = 2
STRIDE = 5
BASE = 128
LANES = 128
UNIT_TILE = 768
VMEM = pl.BlockSpec(memory_space=pltpu.VMEM)
HBM = pl.BlockSpec(memory_space=pl.ANY)
VMEM_LIMIT = 40 * 1024 * 1024


def call(kernel, out_shape, operands, out_spec=VMEM, scratch=(), flops=0, moved=0):
    return pl.pallas_call(
        kernel,
        out_shape=out_shape,
        in_specs=[VMEM] * len(operands),
        out_specs=jax.tree.map(lambda _: out_spec, out_shape),
        scratch_shapes=list(scratch),
        compiler_params=pltpu.CompilerParams(vmem_limit_bytes=VMEM_LIMIT),
        cost_estimate=pl.CostEstimate(flops=flops, bytes_accessed=moved, transcendentals=0),
    )(*operands)


def position_kernel(seq, out_ref):
    shape = (out_ref.shape[0], out_ref.shape[1])
    out_ref[...] = (lax.broadcasted_iota(jnp.int32, shape, 0) % seq).astype(jnp.float32)


def quarter_of(ref, owner, quarter):
    return ref[:, pl.ds(pl.multiple_of(owner * quarter, quarter), quarter)]


def own_kernel(hidden_ref, position_ref, near_ref):
    near_ref[...] = quarter_of(hidden_ref, lax.axis_index("heads"), near_ref.shape[1])


def merge_kernel(hidden_ref, beside_ref, near_ref, far_ref):
    head = lax.axis_index("heads")
    share, quarter = near_ref.shape
    near_ref[...] = quarter_of(beside_ref, head, quarter)
    far_ref[:share, :] = quarter_of(hidden_ref, head ^ 2, quarter)
    far_ref[share:, :] = quarter_of(beside_ref, head ^ 2, quarter)


def gelu(upward):
    return (0.5 * upward * (1.0 + lax.erf(upward * 0.7071067811865476))).astype(jnp.bfloat16)


def feed_forward(hidden_ref, beside_ref, across, weights, gathered, owner):
    head = lax.axis_index("heads")
    share, quarter = hidden_ref.shape[0], gathered.shape[1]
    pieces = (
        quarter_of(hidden_ref, owner, quarter),
        quarter_of(beside_ref, owner, quarter),
        *across,
    )
    for flip, piece in enumerate(pieces):
        rows = pl.ds(pl.multiple_of((head ^ flip) * share, 64), share)
        gathered[rows, :] = piece
    tokens = gathered[...].T
    total = None
    for up_ref, down_ref in weights:
        units = up_ref.shape[1]
        tile = min(UNIT_TILE, units)
        part = None
        for start in range(0, units, tile):
            upward = jnp.dot(
                tokens, up_ref[:, start : start + tile], preferred_element_type=jnp.float32
            )
            term = jnp.dot(
                gelu(upward),
                down_ref[start : start + tile, :],
                preferred_element_type=jnp.float32,
            )
            part = term if part is None else part + term
        part = part.astype(jnp.bfloat16).astype(jnp.float32)
        total = part if total is None else total + part
    return tokens, total


def pair_rows(ref, pair):
    count = ref.shape[0] // 2
    return ref[pl.ds(pl.multiple_of(pair * count, 128), count), :]


def head_rows(ref, head, share):
    return ref[pl.ds(pl.multiple_of(head * share, 64), share), :]


def early_kernel(hidden_ref, beside_ref, u0, u1, out_ref, gathered):
    head = lax.axis_index("heads")
    share, quarter = hidden_ref.shape[0], gathered.shape[1]
    for source, ref in ((head, hidden_ref), (head ^ 1, beside_ref)):
        rows = pl.ds(pl.multiple_of(source % 2 * share, 64), share)
        gathered[rows, :] = quarter_of(ref, head ^ 2, quarter)
    tokens = gathered[...].T
    for i, up_ref in enumerate((u0, u1)):
        out_ref[i] = jnp.dot(
            tokens, pair_rows(up_ref, head // 2), preferred_element_type=jnp.float32
        )


def across_kernel(early_ref, across_ref, u0, u1, out_ref):
    head = lax.axis_index("heads")
    tokens = across_ref[...].T
    for i, up_ref in enumerate((u0, u1)):
        rows = head_rows(up_ref, head ^ 2, tokens.shape[1])
        out_ref[i] = early_ref[i] + jnp.dot(tokens, rows, preferred_element_type=jnp.float32)


def give_kernel(early_ref, diagonal_ref, u0, d0, u1, d1, out_ref):
    head = lax.axis_index("heads")
    tokens = diagonal_ref[...].T
    total = None
    for i, (up_ref, down_ref) in enumerate(((u0, d0), (u1, d1))):
        rows = head_rows(up_ref, head ^ 3, tokens.shape[1])
        upward = early_ref[i] + jnp.dot(tokens, rows, preferred_element_type=jnp.float32)
        part = jnp.dot(gelu(upward), down_ref[...], preferred_element_type=jnp.float32)
        part = part.astype(jnp.bfloat16).astype(jnp.float32)
        total = part if total is None else total + part
    out_ref[...] = total.astype(jnp.bfloat16)


def own_column(values_ref, rows, repeat, first):
    shape = (rows * repeat, values_ref.shape[1])
    wanted = first + lax.broadcasted_iota(jnp.int32, shape, 0) // repeat
    lane = lax.broadcasted_iota(jnp.int32, shape, 1)
    values = values_ref[...].astype(jnp.float32)
    return jnp.sum(jnp.where(lane == wanted, values, 0.0), axis=1, keepdims=True)


def keep_kernel(
    hidden_ref, beside_ref, across_ref, u0, d0, u1, d1, position_ref, length_ref, leaf_ref, parent_ref,
    out_ref, weight_ref, digits_ref, gathered,
):
    head = lax.axis_index("heads")
    rows, lanes = digits_ref.shape
    seq = out_ref.shape[0] // rows
    length = own_column(length_ref, rows, seq, head * rows)
    weight_ref[...] = jnp.where(position_ref[...] < length, 1.0 / length, 0.0)
    lane = lax.broadcasted_iota(jnp.int32, (rows, lanes), 1)
    digits = jnp.zeros((rows, lanes), jnp.int32)
    for at, (ref, first) in enumerate(
        ((leaf_ref, head * rows), (parent_ref, 0), (leaf_ref, (head ^ 1) * rows))
    ):
        values = own_column(ref, rows, 1, first).astype(jnp.int32)
        digits = jnp.where(lane == 2 * at, values % BASE, digits)
        digits = jnp.where(lane == 2 * at + 1, values // BASE, digits)
    digits_ref[...] = digits.astype(jnp.float32)
    weights = ((u0, d0), (u1, d1))
    share = hidden_ref.shape[0]
    across = (across_ref[:share, :], across_ref[share:, :])
    tokens, total = feed_forward(hidden_ref, beside_ref, across, weights, gathered, head)
    out_ref[...] = tokens.astype(jnp.float32) + total


def embed_kernel(kept_ref, came_ref, weight_ref, digits_ref, gain_ref, out_ref):
    rows, width = digits_ref.shape[0], kept_ref.shape[1]
    mixed = (kept_ref[...] + came_ref[...].astype(jnp.float32)).astype(jnp.bfloat16)
    as_float = mixed.astype(jnp.float32)
    centred = as_float - jnp.mean(as_float, axis=1, keepdims=True)
    variance = jnp.mean(centred * centred, axis=1, keepdims=True)
    weight = jnp.concatenate([weight_ref[...]] * (width // LANES), axis=1)
    weighted = centred * weight * lax.rsqrt(variance + 1e-05)
    pooled = jnp.sum(weighted.reshape(rows, -1, width), axis=1) * gain_ref[...]
    scale = lax.rsqrt(jnp.mean(pooled * pooled, axis=1, keepdims=True) + 1e-05)
    both = jnp.concatenate([pooled * scale, digits_ref[...]], axis=1)
    both = both.astype(jnp.bfloat16)
    for i in range(out_ref.shape[0]):
        out_ref[i] = both


def pick_share(values, head, heads):
    share = values.shape[1] // heads
    result = values[:, :share]
    for other in range(1, heads):
        result = jnp.where(head == other, values[:, other * share : (other + 1) * share], result)
    return result


def stride_of(count):
    return STRIDE if count % STRIDE else 1


def position_of(owners, owner, lower):
    half = owners // 2
    place = 2 * ((1 - owner % 2) * half + half - 1 - owner // 2) + lower
    return place * pow(stride_of(2 * owners), -1, 2 * owners) % (2 * owners)


def owner_at(owners, block):
    half = owners // 2
    place = block * stride_of(2 * owners) % owners
    odd = jnp.where(place < half, 1, 0)
    return 2 * (half - 1 - place + (1 - odd) * half) + odd


def own_rows(ref, position, half, rows, width):
    pair = pl.ds(pl.multiple_of(position // 2 * 2 * rows, 2 * rows), 2 * rows)
    return ref[pair, :width].astype(jnp.float32)[half * rows : (half + 1) * rows]


def near_kernel(
    heads, leaf_count, near_ref, sum_ref, share_ref, picker_ref, parent_ref, own_ref
):
    leaves, width = sum_ref.shape
    count = near_ref.shape[0]
    owners = leaves // leaf_count
    digits = near_ref[:, width:].astype(jnp.float32)
    turned = digits.T
    row = lax.broadcasted_iota(jnp.int32, (leaves, count), 0)
    wanted = owner_at(owners, row // leaf_count) * leaf_count + row % leaf_count

    def pick(at):
        leaf = (turned[at : at + 1] + BASE * turned[at + 1 : at + 2]).astype(jnp.int32)
        return jnp.where(wanted == leaf, 1.0, 0.0).astype(jnp.bfloat16)

    near_sum = jnp.dot(pick(0), near_ref[:, :width], preferred_element_type=jnp.float32)
    sum_ref[...] = near_sum
    share_ref[...] = pick_share(near_sum, lax.axis_index("heads"), heads)
    picker_ref[...] = pick(4)
    digits = digits.reshape(owners, count // owners, LANES)[:, :leaf_count].reshape(leaves, LANES)
    parent = digits[:, 2:3] + BASE * digits[:, 3:4]
    parent_ref[...] = jnp.broadcast_to(parent, parent_ref.shape)
    rows = own_ref.shape[0] // 2
    for i in range(2):
        position = position_of(owners, lax.axis_index("labels"), 1 - i)
        own_ref[i * rows : (i + 1) * rows, :] = own_rows(near_ref, position, 1 - i, rows, width)


def leaf_kernel(
    heads, far_ref, sum_ref, share_ref, picker_ref, parent_ref, own_ref,
    embed_out, centers_out, parents_out, embed_ref, centers_ref, parents_ref, scratch, sems,
):
    head, index = lax.axis_index("heads"), lax.axis_index("labels")
    core = head % 2
    width = embed_ref.shape[1]
    rows = embed_ref.shape[0] // heads
    leaf_count = centers_ref.shape[0]
    owners = sum_ref.shape[0] // leaf_count
    upper, lower = position_of(owners, index, 0), position_of(owners, index, 1)

    blocks = []
    for i, position in enumerate((lower, upper)):
        near = own_ref[i * rows : (i + 1) * rows, :]
        far = own_rows(far_ref, position, 1 - i, rows, width)
        blocks += [jnp.where(core == 0, near, far), jnp.where(core == 0, far, near)]
    embed_ref[...] = jnp.concatenate(blocks, axis=0).astype(jnp.bfloat16)
    embed_copy = pltpu.make_async_copy(embed_ref, embed_out, sems.at[0])
    embed_copy.start()
    picker = picker_ref[...]
    leaf_sum = sum_ref[...] + jnp.dot(
        picker, far_ref[:, :width], preferred_element_type=jnp.float32
    )
    far_share = pick_share(far_ref[:, :width], head, heads)
    leaf_share = share_ref[...] + jnp.dot(picker, far_share, preferred_element_type=jnp.float32)
    squares = jnp.mean(leaf_sum * leaf_sum, axis=1, keepdims=True)
    centers = leaf_share * lax.rsqrt(squares + 1e-05)
    parent = parent_ref[:, :1].astype(jnp.int32)
    sums = [
        jnp.sum(jnp.where(parent == index * PAR_DEV + p, centers, 0.0), axis=0, keepdims=True)
        for p in range(PAR_DEV)
    ]
    parents_ref[...] = jnp.concatenate(sums, axis=0)
    parents_copy = pltpu.make_async_copy(parents_ref, parents_out, sems.at[2])
    parents_copy.start()
    scratch[...] = centers
    own = pl.ds(pl.multiple_of(upper // 2 * leaf_count, leaf_count), leaf_count)
    centers_ref[...] = scratch[own, :]
    centers_copy = pltpu.make_async_copy(centers_ref, centers_out, sems.at[1])
    centers_copy.start()
    embed_copy.wait()
    centers_copy.wait()
    parents_copy.wait()


def local(owners, heads, hidden_in, w_up, w_down, norm_gain, title_length, label_leaf, leaf_parent):
    token_rows, share = hidden_in.shape
    width = w_down.shape[1]
    units = w_up.shape[1]
    labels_here = label_leaf.shape[0]
    leaf_count = leaf_parent.shape[0]
    rows = labels_here // heads
    quarter = token_rows // heads

    def swap(values, flip):
        return lax.ppermute(values, "heads", [(i, i ^ flip) for i in range(heads)])

    def array(*shape, dtype=jnp.float32):
        return jax.ShapeDtypeStruct(shape, dtype)

    hidden = hidden_in.T
    beside = swap(hidden, 1)
    position = call(
        functools.partial(position_kernel, token_rows // labels_here),
        array(quarter, LANES),
        (),
        flops=5000000000,
    )
    up_far, down_far = swap(w_up, 1), swap(w_down, 1)
    piece = array(share, quarter, dtype=jnp.bfloat16)
    across = swap(call(own_kernel, piece, (hidden, position), flops=5000000000), 2)
    near, far = call(
        merge_kernel,
        (piece, array(2 * share, quarter, dtype=jnp.bfloat16)),
        (hidden, beside),
        flops=10000000000,
    )
    diagonal = swap(near, 2)
    come_keep = swap(far, 2)
    weights = (w_up, w_down, up_far, down_far)
    cost = dict(
        scratch=[pltpu.VMEM((width, quarter), jnp.bfloat16)],
        flops=8 * quarter * width * units,
        moved=8 * width * units,
    )
    upward = array(2, quarter, units)
    early = call(
        early_kernel,
        upward,
        (hidden, beside, w_up, up_far),
        scratch=[pltpu.VMEM((width // 2, quarter), jnp.bfloat16)],
    )
    early = call(across_kernel, upward, (early, across, w_up, up_far), flops=0)
    given = call(
        give_kernel,
        array(quarter, width, dtype=jnp.bfloat16),
        (early, diagonal, *weights),
        flops=8 * quarter * width * units,
        moved=8 * width * units,
    )
    came = swap(given, 2)
    kept, weight, digits = call(
        keep_kernel,
        (array(quarter, width), array(quarter, LANES), array(rows, LANES)),
        (
            *(hidden, beside, come_keep, *weights, position),
            *(title_length[None, :], label_leaf[None, :], leaf_parent[None, :]),
        ),
        **dict(cost, flops=10_000_000_000),
    )
    message = call(
        embed_kernel,
        array(owners * heads // 2, rows, width + LANES, dtype=jnp.bfloat16),
        (kept, came, weight, digits, norm_gain[None, :]),
    )
    groups = [
        sorted(
            range(core, owners * heads, 2),
            key=lambda rank: position_of(owners, rank // heads, 1 - rank % heads // 2),
        )
        for core in range(2)
    ]
    members = owners * heads // 2
    near = lax.all_to_all(
        message,
        ("labels", "heads"),
        split_axis=0,
        concat_axis=0,
        tiled=True,
        axis_index_groups=groups,
    ).reshape(members * rows, width + LANES)
    far = swap(near, 1)
    leaves = owners * leaf_count
    ready = call(
        functools.partial(near_kernel, heads, leaf_count),
        (
            array(leaves, width),
            array(leaves, share),
            array(leaves, members * rows, dtype=jnp.bfloat16),
            array(leaves, LANES),
            array(2 * rows, width),
        ),
        (near,),
    )
    outputs = (
        array(labels_here, width, dtype=jnp.bfloat16),
        array(leaf_count, share),
        array(PAR_DEV, share),
    )
    return call(
        functools.partial(leaf_kernel, heads),
        outputs,
        (far, *ready),
        out_spec=HBM,
        scratch=[pltpu.VMEM(out.shape, out.dtype) for out in outputs]
        + [pltpu.VMEM((leaves, share), jnp.float32), pltpu.SemaphoreType.DMA((3,))],
    )


def solution(mesh):
    in_specs = (
        P("labels", "heads"),
        P(None, "heads"),
        P("heads", None),
        P(),
        P("labels"),
        P("labels"),
        P("labels"),
    )
    out_specs = (P("labels", None), P("labels", "heads"), P("labels", "heads"))
    body = functools.partial(local, mesh.shape["labels"], mesh.shape["heads"])
    return jax.shard_map(body, mesh=mesh, in_specs=in_specs, out_specs=out_specs, check_vma=False)
```
